128 devices in a mesh: row: 4 (over y), col: 32 (over z, x, core).
Axes of the slice: x: 4, y: 4, z: 4, core: 2. Of those that a mesh axis runs over, the one named last changes fastest.
Arguments:
- boundary: bfloat16 [32, 4, 128, 8, 128], P('col'), may hold values from -6 to 6
- peps_rows: bfloat16 [4, 32, 8, 8, 8, 8], P('row', 'col'), may hold values from -2 to 2
- sketch: bfloat16 [4, 32, 4, 1024, 128], P('row', 'col'), may hold values from -0.1875 to 0.1875
- ranks: int32 [4, 32, 4], P('row', 'col'), may hold values from 64 to 128
- sizes: int32 [4], replicated, may hold values from 64 to 128
- charges: int32 [8], replicated, may hold values from -1 to 1
Outputs:
- absorbed: bfloat16 [4, 32, 4, 128, 8, 128], P('row', 'col')
The draws below stay inside these ranges and needn't reach their ends.
All inputs are finite; a program needn't handle non-finite values.
Results may differ from the reference program's by a relative error of at most 0.03.
Values may be sent and summed in bfloat16 or wider, within the bound.
A program may use at most 128 MiB of HBM per device.

```python
from functools import partial
import jax
import jax.numpy as jnp
from jax import lax

W = 128
D = 8
NS = 4
RPS = 1
COLS = 32
ROWS = 4


def touch_ends(values, key, smallest, top_value):
    spot = [jax.random.randint(jax.random.fold_in(key, axis), (), 0, length) for axis, length in enumerate(values.shape)]
    main_axis = values.shape.index(max(values.shape))
    beside = spot[:main_axis] + [(spot[main_axis] + 1) % values.shape[main_axis]] + spot[main_axis + 1:]
    return values.at[tuple(spot)].set(smallest).at[tuple(beside)].set(top_value)


def shard_levels(key, dims, shards, least, top_value):
    level = 1.0
    for position, shards_of in shards:
        steps = jax.random.uniform(jax.random.fold_in(jax.random.fold_in(key, 6), position), (shards_of,), jnp.float32, least / len(shards), top_value / len(shards))
        level = level * jnp.repeat(jnp.exp(steps), dims[position] // shards_of).reshape((-1,) + (1,) * (len(dims) - 1 - position))
    return level


def scatter_about(stream_key, dims, scale, bound, cuts=(), kind=jnp.bfloat16):
    factor_of = shard_levels(stream_key, dims, cuts, -0.22, 0.18) if cuts else 1.0
    drawn = jax.random.normal(stream_key, dims, jnp.float32) * scale * factor_of
    return jnp.minimum(jnp.maximum(drawn, -bound), bound).astype(kind)


def setup_inputs(seed: int = 0) -> dict:
    splits = jax.random.split(jax.random.key(seed), 7)
    boundary = scatter_about(splits[0], (COLS, NS, W, D, W), 1.0, 6.0, ((0, 32),))
    peps_rows = scatter_about(splits[1], (ROWS, COLS, D, D, D, D), D ** -0.5, 2.0, ((0, 4), (1, 32)))
    sketch = scatter_about(splits[2], (ROWS, COLS, NS, W * D, W), (W * D) ** -0.5, 0.1875, ((0, 4), (1, 32)))
    ranks = touch_ends(jax.random.randint(splits[3], (ROWS, COLS, NS), W // 2, W + 1), jax.random.fold_in(splits[3], 1), W // 2, W).astype(jnp.int32)
    sizes = touch_ends(jax.random.randint(splits[4], (NS,), W // 2, W + 1), jax.random.fold_in(splits[4], 1), W // 2, W).astype(jnp.int32)
    charges = touch_ends(jax.random.randint(splits[5], (D,), -1, 2), jax.random.fold_in(splits[5], 1), -1, 1).astype(jnp.int32)
    return dict(boundary=boundary, peps_rows=peps_rows, sketch=sketch, ranks=ranks, sizes=sizes, charges=charges)


def to_float(values):
    return values.astype(jnp.float32)

def sketch_column(blocks, tensor, right_sketch, left_sketch):
    top = lax.Precision.HIGHEST
    bond_sketch = jnp.einsum('saub,sbrk->saurk', to_float(blocks), to_float(right_sketch), precision=top).astype(jnp.bfloat16)
    left_side = jnp.einsum('saurk,lrud->saldk', to_float(bond_sketch), to_float(tensor), precision=top).astype(jnp.bfloat16)
    edge_sketch = jnp.einsum('salk,saub->sklub', to_float(left_sketch), to_float(blocks), precision=top).astype(jnp.bfloat16)
    right_side = jnp.einsum('sklub,lrud->skdrb', to_float(edge_sketch), to_float(tensor), precision=top).astype(jnp.bfloat16)
    gram_left = jnp.einsum('saldk,saldm->skm', to_float(left_side), to_float(left_side), precision=top)
    gram_right = jnp.einsum('skdrb,smdrb->skm', to_float(right_side), to_float(right_side), precision=top)
    middle = jnp.einsum('salk,saldm->skdm', to_float(left_sketch), to_float(left_side), precision=top)
    return (gram_left, gram_right, middle)

def finish_column(middle, left_factor, right_factor):
    sectors, tile_width, bond_depth, _ = middle.shape
    solver = jax.vmap(partial(jax.scipy.linalg.solve_triangular, lower=True))
    flattened = middle.reshape(sectors, tile_width, bond_depth * tile_width)
    lefted = solver(left_factor, flattened).reshape(sectors, tile_width, bond_depth, tile_width)
    turned = jnp.transpose(lefted, (0, 3, 1, 2)).reshape(sectors, tile_width, tile_width * bond_depth)
    righted = solver(right_factor, turned).reshape(sectors, tile_width, tile_width, bond_depth)
    result = jnp.transpose(righted, (0, 2, 3, 1))
    scaling = lax.rsqrt(lax.optimization_barrier(jnp.mean(result * result, axis=(1, 2, 3), keepdims=True)) + 1e-06)
    return (result * scaling).astype(jnp.bfloat16)

def reference(boundary, peps_rows, sketch, ranks, sizes, charges):
    positions = jnp.arange(W, dtype=jnp.int32)
    inside = (positions[None, :] < sizes[:, None]).astype(boundary.dtype)
    blocks = boundary * inside[None, :, :, None, None] * inside[None, :, None, None, :]
    conserved = charges[:, None, None, None] + charges[None, None, :, None] == charges[None, :, None, None] + charges[None, None, None, :]
    tensors = jnp.where(conserved[None, None], peps_rows, jnp.zeros_like(peps_rows))
    kept_mask = (positions[None, None, None, :] < ranks[:, :, :, None]).astype(sketch.dtype)
    sketches = sketch.reshape(ROWS, COLS, NS, W, D, W) * kept_mask[:, :, :, None, None, :]
    identity = jnp.eye(W, dtype=jnp.float32)
    stored = []
    for row_index in range(ROWS):
        right_sketch = sketches[row_index]
        left_sketch = jnp.roll(right_sketch, 1, axis=0)
        grams_left, grams_right, middles = lax.map(lambda operands: sketch_column(*operands), (blocks, tensors[row_index], right_sketch, left_sketch))
        bond_matrices = grams_left + jnp.roll(grams_right, -1, axis=0) + identity
        factors = jnp.linalg.cholesky(bond_matrices)
        blocks = lax.map(lambda operands: finish_column(*operands), (middles, jnp.roll(factors, 1, axis=0), factors))
        if (row_index + 1) % RPS == 0:
            stored.append(blocks)
    return jnp.stack(stored)
```

```python
import functools

import jax
import jax.numpy as jnp
from jax import lax
from jax.experimental import pallas as pl
from jax.experimental.pallas import tpu as pltpu
from jax.sharding import PartitionSpec as P

W = 128
D = 8
NS = 4
F32 = jnp.float32
BF16 = jnp.bfloat16
TOP = lax.Precision.HIGHEST
MESH = pl.DeviceIdType.MESH


def iota(shape, axis):
    return lax.broadcasted_iota(jnp.int32, shape, axis)


def mm(a, b, precision=None):
    return jnp.dot(a, b, preferred_element_type=F32, precision=precision)


def mm_nt(a, b, precision=None):
    return lax.dot_general(
        a, b, (((1,), (1,)), ((), ())), preferred_element_type=F32, precision=precision
    )


def mm_tn(a, b, precision=None):
    return lax.dot_general(
        a, b, (((0,), (0,)), ((), ())), preferred_element_type=F32, precision=precision
    )


def compact_tensor(peps_ref, charges_ref, compact):
    rows = iota((512, 1), 0)
    l, h, u = rows >> 6, (rows >> 3) & 7, rows & 7
    balance = jnp.zeros((512, 1), jnp.int32)
    for i in range(D):
        q = charges_ref[i]
        balance += q * (
            (l == i).astype(jnp.int32) + (u == i).astype(jnp.int32) - (h == i).astype(jnp.int32)
        )
    values = peps_ref[...].astype(F32).reshape(512, D)
    big = iota((512, 256), 0)
    lane = iota((512, 256), 1) & 63
    same_hu = (big & 63) == lane
    same_lu = (((big >> 6) << 3) | (big & 7)) == lane
    pick = iota((D, 512), 0)
    from_row = iota((D, 512), 1)
    pick_l = (pick == (from_row >> 6)).astype(BF16)
    pick_h = (pick == ((from_row >> 3) & 7)).astype(BF16)
    for d in range(D):
        column = jnp.where(balance == charges_ref[d], values[:, d : d + 1], 0.0)
        spread = jnp.broadcast_to(column, (512, 256))
        compact[0, pl.ds(d * D, D), :] = mm(pick_l, jnp.where(same_hu, spread, 0.0).astype(BF16))
        compact[1, pl.ds(d * D, D), :] = mm(pick_h, jnp.where(same_lu, spread, 0.0).astype(BF16))


def inverse_factors(work, inverse):
    row = iota((8, 256), 0)
    lane = iota((8, 256), 1)
    for p in range(W // 8):
        for i in range(2):
            panel = work[i, pl.ds(8 * p, 8), :]
            for t in range(7):
                j = 8 * p + t
                column = panel[:, j : j + 1]
                factor = column / panel[t : t + 1, j : j + 1]
                panel = panel - jnp.where(row > t, factor, 0.0) * panel[t : t + 1, :]
            pivots = jnp.sum(jnp.where(lane == row + 8 * p, panel, 0.0), axis=1, keepdims=True)
            panel = panel * lax.rsqrt(pivots)
            inverse[i, pl.ds(8 * p, 8), :] = panel[:, W:]
            if p < W // 8 - 1:
                update = mm_tn(panel[:, :W], panel, TOP)
                work[i, pl.ds(8 * p + 8, W - 8 * p - 8), :] -= update[8 * p + 8 :, :]


def kernel(
    peps_ref, ranks_ref, sizes_ref, charges_ref, boundary_ref, sketch_ref, out_ref,
    sk, bm, bt, r_raw, l_raw, r_wide, l_wide, l_turned, comp32, comp, kron, z, z2, mid, tall,
    gram_own, gl_out, gr_out, gl_in, gr_in, work, inverse,
    sk_sem, b_sem, r_send, r_recv, w_send, w_recv, l_send, l_recv,
    gl_send, gl_recv, gr_send, gr_recv, o_send, o_recv, o_local,
):
    me = lax.axis_index("row")
    col = lax.axis_index("col")
    cols = lax.axis_size("col")
    right = lax.rem(col + 1, cols)
    left = lax.rem(col + cols - 1, cols)

    def sketch_load(s):
        return pltpu.make_async_copy(sketch_ref.at[s], sk.at[s], sk_sem.at[s])

    for s in range(NS):
        sketch_load(s).start()
    boundary_load = pltpu.make_async_copy(boundary_ref.at[me], bm.at[0], b_sem)
    boundary_load.start()

    barrier = pltpu.get_barrier_semaphore()
    for k in range(1, NS):
        pl.semaphore_signal(
            barrier, inc=1, device_id=(lax.rem(me + k, NS), col), device_id_type=MESH
        )
    for c in (left, right):
        pl.semaphore_signal(barrier, inc=1, device_id=(me, c), device_id_type=MESH)
    pl.semaphore_wait(barrier, NS + 1)

    lanes = iota((1, W), 1)
    for s in range(NS):
        sketch_load(s).wait()
        kept = (lanes < ranks_ref[s]).astype(BF16)
        sk[s] = sk[s] * kept
    r_raw[me] = sk[me]

    def r_copy(k):
        s = lax.rem(me + k, NS)
        return pltpu.make_async_remote_copy(
            src_ref=sk.at[s], dst_ref=r_raw.at[me], send_sem=r_send.at[k - 1],
            recv_sem=r_recv.at[me], device_id=(s, col), device_id_type=MESH,
        )

    def r_arrival(r):
        return pltpu.make_async_remote_copy(
            src_ref=sk.at[0], dst_ref=r_raw.at[r], send_sem=r_send.at[0],
            recv_sem=r_recv.at[r], device_id=(me, col), device_id_type=MESH,
        )

    def w_copy(k):
        s = lax.rem(me + k, NS)
        return pltpu.make_async_remote_copy(
            src_ref=comp.at[me], dst_ref=comp.at[me], send_sem=w_send.at[k - 1],
            recv_sem=w_recv.at[me], device_id=(s, col), device_id_type=MESH,
        )

    def w_arrival(r):
        return pltpu.make_async_remote_copy(
            src_ref=comp.at[r], dst_ref=comp.at[r], send_sem=w_send.at[0],
            recv_sem=w_recv.at[r], device_id=(me, col), device_id_type=MESH,
        )

    def l_copy(r):
        return pltpu.make_async_remote_copy(
            src_ref=r_raw.at[r], dst_ref=l_raw.at[r], send_sem=l_send.at[r],
            recv_sem=l_recv.at[r], device_id=(me, right), device_id_type=MESH,
        )

    def gl_copy(r):
        return pltpu.make_async_remote_copy(
            src_ref=gl_out.at[r], dst_ref=gl_in.at[r], send_sem=gl_send.at[r],
            recv_sem=gl_recv.at[r], device_id=(me, right), device_id_type=MESH,
        )

    def gr_copy(r):
        return pltpu.make_async_remote_copy(
            src_ref=gr_out.at[r], dst_ref=gr_in.at[r], send_sem=gr_send.at[r],
            recv_sem=gr_recv.at[r], device_id=(me, left), device_id_type=MESH,
        )

    def o_copy(r):
        return pltpu.make_async_remote_copy(
            src_ref=bm.at[r + 1], dst_ref=out_ref.at[me], send_sem=o_send.at[r],
            recv_sem=o_recv.at[me], device_id=(r, col), device_id_type=MESH,
        )

    def o_arrival(s):
        return pltpu.make_async_remote_copy(
            src_ref=bm.at[1], dst_ref=out_ref.at[s], send_sem=o_send.at[0],
            recv_sem=o_recv.at[s], device_id=(me, col), device_id_type=MESH,
        )

    def o_stay(r):
        return pltpu.make_async_copy(bm.at[r + 1], out_ref.at[me], o_local)

    @pl.when(me == 0)
    def _():
        for k in (2, 1, 3):
            r_copy(k).start()

    compact_tensor(peps_ref, charges_ref, comp32)
    comp[me] = comp32[...].astype(BF16)
    for k in range(1, NS):
        w_copy(k).start()

    size = sizes_ref[me]
    boundary_load.wait()
    start = jnp.where(
        ((iota((W * D, W), 0) >> 3) < size) & (iota((W * D, W), 1) < size),
        bm[0].astype(F32), 0.0,
    )
    bm[0] = start.astype(BF16)
    tall[...] = start
    for u in range(D):
        mid[:, u * W : (u + 1) * W] = tall[pl.ds(u, W, stride=D), :].T
    for u in range(D):
        tall[pl.ds(u, W, stride=D), :] = mid[:, u * W : (u + 1) * W]
    bt[...] = tall[...].astype(BF16)

    block = iota((256, 256), 0) >> 6 == iota((256, 256), 1) >> 6

    def prepare(r):
        @pl.when(r != me)
        def _():
            r_arrival(r).wait_recv()

        l_copy(r).start()

        @pl.when((r == 0) & (me != 0))
        def _():
            for k in (2, 1, 3):
                r_copy(k).start()

        tall[...] = r_raw[r].astype(F32)
        for h in range(D):
            r_wide[:, h * W : (h + 1) * W] = tall[pl.ds(h, W, stride=D), :].astype(BF16)

        @pl.when(r != me)
        def _():
            w_arrival(r).wait_recv()

        for i in range(2):
            one = comp[r, i]
            kron[i] = jnp.where(block, jnp.concatenate([one] * 4, axis=0).astype(F32), 0.0).astype(
                BF16
            )
        l_copy(r).wait_recv()
        natural = l_raw[r].astype(F32)
        tall[...] = natural
        for h in range(D):
            l_wide[:, h * W : (h + 1) * W] = tall[pl.ds(h, W, stride=D), :].astype(BF16)
        l_turned[...] = natural.T.astype(BF16)

    def sided(lhs, wide, tensor, store):
        for g in range(W // 16):
            part = mm(lhs[pl.ds(g * 128, 128), :], wide)
            columns = []
            for q in range(4):
                pieces = [
                    part[(4 * q + i) * D : (4 * q + i + 1) * D, h * W : (h + 1) * W]
                    for i in range(4)
                    for h in range(D)
                ]
                columns.append(jnp.concatenate(pieces, axis=0).astype(BF16))
            side = mm(tensor, jnp.concatenate(columns, axis=1))
            store(g, side)

    def store_left(g, side):
        for d in range(D):
            pieces = [
                side[(i * D + d) * D : (i * D + d + 1) * D, q * W : (q + 1) * W]
                for q in range(4)
                for i in range(4)
            ]
            z[pl.ds(g * 128, 128), d * W : (d + 1) * W] = jnp.concatenate(pieces, axis=0).astype(
                BF16
            )

    def store_right(g, side):
        z2[g] = side.astype(BF16)

    prepare(0)

    def absorb(r, carry):
        sided(bm.at[r], r_wide[...], kron[0], store_left)
        gram = jnp.zeros((W, W), F32)
        for d in range(D):
            piece = z[:, d * W : (d + 1) * W]
            gram += mm_tn(piece, piece)
        gram_own[0] = gram
        gl_out[r] = gram.astype(BF16)
        gl_copy(r).start()
        sided(bt, l_wide[...], kron[1], store_right)
        gram = jnp.zeros((W, W), F32)
        for g in range(W // 16):
            for q in range(4):
                piece = z2[g, :, q * W : (q + 1) * W]
                gram += mm_tn(piece, piece)
        gram_own[1] = gram
        gr_out[r] = gram.astype(BF16)
        gr_copy(r).start()
        mid[...] = mm(l_turned[...], z[...])

        @pl.when(r < NS - 1)
        def _():
            prepare(r + 1)

        eye = (iota((W, W), 0) == iota((W, W), 1)).astype(F32)
        gl_copy(r).wait_recv()
        gr_copy(r).wait_recv()
        work[0, :, :W] = gl_in[r].astype(F32) + gram_own[1] + eye
        work[1, :, :W] = gr_in[r].astype(F32) + gram_own[0] + eye
        work[0, :, W:] = eye
        work[1, :, W:] = eye
        inverse_factors(work, inverse)
        lefted = mm(inverse[0], mid[...], TOP)
        for d in range(D):
            tall[pl.ds(d, W, stride=D), :] = lefted[:, d * W : (d + 1) * W]
        fresh = mm_nt(tall[...], inverse[1], TOP)
        scaling = lax.rsqrt(jnp.mean(fresh * fresh) + 1e-6)
        bm[r + 1] = (fresh * scaling).astype(BF16)

        @pl.when(r != me)
        def _():
            o_copy(r).start()

        @pl.when(r == me)
        def _():
            o_stay(r).start()

        @pl.when(r < NS - 1)
        def _():
            for d in range(D):
                tall[pl.ds(d, W, stride=D), :] = mm_nt(
                    inverse[1], lefted[:, d * W : (d + 1) * W], TOP
                )
            bt[...] = (tall[...] * scaling).astype(BF16)

        return carry

    lax.fori_loop(0, NS, absorb, 0)

    for k in range(1, NS):
        r_copy(k).wait_send()
        w_copy(k).wait_send()
    for r in range(NS):
        l_copy(r).wait_send()
        gl_copy(r).wait_send()
        gr_copy(r).wait_send()
    for r in range(NS):

        @pl.when(r != me)
        def _():
            o_copy(r).wait_send()
            o_arrival(r).wait_recv()

    o_stay(me).wait()


def body(boundary, peps_rows, sketch, ranks, sizes, charges):
    any_space = pl.BlockSpec(memory_space=pl.ANY)
    smem = pl.BlockSpec(memory_space=pltpu.SMEM)
    vmem = pl.BlockSpec(memory_space=pltpu.VMEM)
    dma = pltpu.SemaphoreType.DMA
    result = pl.pallas_call(
        kernel,
        out_shape=jax.ShapeDtypeStruct((NS, W * D, W), BF16),
        in_specs=[vmem, smem, smem, smem, any_space, any_space],
        out_specs=any_space,
        scratch_shapes=[
            pltpu.VMEM((NS, W * D, W), BF16),
            pltpu.VMEM((NS + 1, W * D, W), BF16),
            pltpu.VMEM((W * D, W), BF16),
            pltpu.VMEM((NS, W * D, W), BF16),
            pltpu.VMEM((NS, W * D, W), BF16),
            pltpu.VMEM((W, W * D), BF16),
            pltpu.VMEM((W, W * D), BF16),
            pltpu.VMEM((W, W * D), BF16),
            pltpu.VMEM((2, 64, 256), F32),
            pltpu.VMEM((NS, 2, 64, 256), BF16),
            pltpu.VMEM((2, 256, 256), BF16),
            pltpu.VMEM((W * D, W * D), BF16),
            pltpu.VMEM((W // 16, 256, 4 * W), BF16),
            pltpu.VMEM((W, W * D), F32),
            pltpu.VMEM((W * D, W), F32),
            pltpu.VMEM((2, W, W), F32),
            pltpu.VMEM((NS, W, W), BF16),
            pltpu.VMEM((NS, W, W), BF16),
            pltpu.VMEM((NS, W, W), BF16),
            pltpu.VMEM((NS, W, W), BF16),
            pltpu.VMEM((2, W, 2 * W), F32),
            pltpu.VMEM((2, W, W), F32),
            dma((NS,)), dma(()), dma((NS - 1,)), dma((NS,)), dma((NS - 1,)), dma((NS,)),
            dma((NS,)), dma((NS,)), dma((NS,)), dma((NS,)), dma((NS,)), dma((NS,)),
            dma((NS,)), dma((NS,)), dma(()),
        ],
        compiler_params=pltpu.CompilerParams(
            collective_id=0, has_side_effects=True, vmem_limit_bytes=56 * 2**20
        ),
        name="absorb_rows",
    )(
        peps_rows.reshape(D * D, D, D),
        ranks.reshape(NS),
        sizes,
        charges,
        boundary.reshape(NS, W * D, W),
        sketch.reshape(NS, W * D, W),
    )
    return result.reshape(1, 1, NS, W, D, W)


def solution(mesh):
    placed = (
        P("col", None, None, None, None),
        P("row", "col", None, None, None, None),
        P("row", "col", None, None, None),
        P("row", "col", None),
        P(),
        P(),
    )
    return jax.shard_map(
        body,
        mesh=mesh,
        in_specs=placed,
        out_specs=P("row", "col", None, None, None, None),
        check_vma=False,
    )
```

```python
import jax
import jax.numpy as jnp
from jax import lax
from jax.experimental import pallas as pl
from jax.experimental.pallas import tpu as pltpu
from jax.sharding import PartitionSpec as P

W = 128
D = 8
NS = 4
F32 = jnp.float32
BF16 = jnp.bfloat16
MESH = pl.DeviceIdType.MESH


def iota(shape, axis):
    return lax.broadcasted_iota(jnp.int32, shape, axis)


def mm(a, b):
    return jnp.dot(a, b, preferred_element_type=F32)


def mm_nt(a, b):
    return lax.dot_general(a, b, (((1,), (1,)), ((), ())), preferred_element_type=F32)


def mm_tn(a, b):
    return lax.dot_general(a, b, (((0,), (0,)), ((), ())), preferred_element_type=F32)


def compact_tensor(peps_ref, charges_ref, compact):
    rows = iota((512, 1), 0)
    l, h, u = rows >> 6, (rows >> 3) & 7, rows & 7
    balance = jnp.zeros((512, 1), jnp.int32)
    for i in range(D):
        q = charges_ref[i]
        balance += q * (
            (l == i).astype(jnp.int32) + (u == i).astype(jnp.int32) - (h == i).astype(jnp.int32)
        )
    values = peps_ref[...].astype(F32).reshape(512, D)
    big = iota((512, 256), 0)
    lane = iota((512, 256), 1) & 63
    same_hu = (big & 63) == lane
    same_lu = (((big >> 6) << 3) | (big & 7)) == lane
    pick = iota((D, 512), 0)
    from_row = iota((D, 512), 1)
    pick_l = (pick == (from_row >> 6)).astype(BF16)
    pick_h = (pick == ((from_row >> 3) & 7)).astype(BF16)
    for d in range(D):
        column = jnp.where(balance == charges_ref[d], values[:, d : d + 1], 0.0)
        spread = jnp.broadcast_to(column, (512, 256))
        compact[0, pl.ds(d * D, D), :] = mm(pick_l, jnp.where(same_hu, spread, 0.0).astype(BF16))
        compact[1, pl.ds(d * D, D), :] = mm(pick_h, jnp.where(same_lu, spread, 0.0).astype(BF16))


def halves(x):
    high = x.astype(BF16)
    return high, (x - high.astype(F32)).astype(BF16)


def mm3(a, b):
    ah, al = halves(a)
    bh, bl = halves(b)
    return mm(jnp.concatenate([ah, ah, al], axis=1), jnp.concatenate([bh, bl, bh], axis=0))


def mm3_tn(a, b):
    ah, al = halves(a)
    bh, bl = halves(b)
    return mm_tn(jnp.concatenate([ah, ah, al], axis=0), jnp.concatenate([bh, bl, bh], axis=0))


def vreg(x):
    return jnp.broadcast_to(x, (8, W))


def eliminate(tiles, first, part):
    sub = iota((8, W), 0)
    tiles = list(tiles)

    def spread(v, j):
        a, b = (first[0] + j) % W, (first[1] + j) % W
        return jnp.where(part, vreg(v[:, a : a + 1]), vreg(v[:, b : b + 1]))

    for q in range(4):
        columns = [spread(tiles[q], 8 * q + t) for t in range(8)]
        s = {(i, t): vreg(columns[t][i : i + 1, :]) for t in range(8) for i in range(t, 8)}
        low = {o: [spread(tiles[o], 8 * q + t) for t in range(8)] for o in range(q + 1, 4)}
        f, n, root = {}, {}, []
        for t in range(8):
            root.append(lax.rsqrt(s[t, t]))
            over = root[t] * root[t]
            for i in range(t + 1, 8):
                f[i, t] = s[i, t] * over
                for k in range(t + 1, i + 1):
                    s[i, k] = s[i, k] - (s[i, t] * s[k, t]) * over
        for j in range(8):
            for i in range(j + 1, 8):
                total = f[i, j]
                for k in range(j + 1, i):
                    total = total + f[i, k] * n[k, j]
                n[i, j] = -total
        g = {
            (i, j): (root[i] if i == j else n[i, j] * root[i])
            for j in range(8)
            for i in range(j, 8)
        }
        panel, result = tiles[q], None
        for j in range(8):
            column = jnp.zeros((8, W), F32)
            for i in range(j, 8):
                column = jnp.where(sub == i, g[i, j], column)
            term = column * vreg(panel[j : j + 1, :])
            result = term if result is None else result + term
        tiles[q] = result
        for o in range(q + 1, 4):
            rest = tiles[o]
            for t in range(8):
                factor = None
                for j in range(t + 1):
                    term = low[o][j] * g[t, j]
                    factor = term if factor is None else factor + term
                rest = rest - factor * vreg(result[t : t + 1, :])
            tiles[o] = rest
    return tiles


def inverse_factors(work, inverse, mixed):
    lane, sub = iota((8, W), 1), iota((8, W), 0)
    group = lane >> 5
    for k in range(4):
        at = [(k + i) % 4 for i in range(4)]
        part = (group == at[0]) | (group == at[1])
        tiles = []
        for q in range(4):
            rows = pl.ds(32 * k + 8 * q, 8)
            one = work[0, rows, :W]
            two = pltpu.roll(work[1, rows, :W], 64, 1)
            unit = ((lane & 31) == (sub + 8 * q)).astype(F32)
            tiles.append(jnp.where(group == at[0], one, jnp.where(group == at[2], two, unit)))
        done = jnp.concatenate(eliminate(tiles, (32 * k, 32 * k + 64), part), axis=0)
        mixed[...] = jnp.zeros((W, 4 * W), F32)
        mixed[pl.ds(32 * at[1], 32), : 2 * W] = work[0, pl.ds(32 * k, 32), :]
        mixed[pl.ds(32 * at[3], 32), 2 * W :] = work[1, pl.ds(32 * k, 32), :]
        both = mm3(done, mixed[...])
        for i in range(2):
            panel = both[:, i * 2 * W : (i + 1) * 2 * W]
            inverse[i, pl.ds(32 * k, 32), :] = panel[:, W:]
            if k < 3:
                below = 32 * (k + 1)
                update = mm3_tn(panel[:, :W], panel)
                work[i, pl.ds(below, W - below), :] -= update[below:, :]


def kernel(
    peps_ref, ranks_ref, sizes_ref, charges_ref, boundary_ref, sketch_ref, out_ref,
    sk, bm, bt, r_raw, l_raw, r_wide, l_wide, l_turned, comp32, comp, kron, z, z2, mid, tall,
    gram_own, gl_out, gr_out, gl_in, gr_in, work, inverse, mixed,
    sk_sem, b_sem, r_send, r_recv, w_send, w_recv, l_send, l_recv,
    gl_send, gl_recv, gr_send, gr_recv, o_send, o_recv, o_local,
):
    me = lax.axis_index("row")
    col = lax.axis_index("col")
    cols = lax.axis_size("col")
    right = lax.rem(col + 1, cols)
    left = lax.rem(col + cols - 1, cols)

    def sketch_load(s):
        return pltpu.make_async_copy(sketch_ref.at[s], sk.at[s], sk_sem.at[s])

    for s in range(NS):
        sketch_load(s).start()
    boundary_load = pltpu.make_async_copy(boundary_ref.at[me], bm.at[0], b_sem)
    boundary_load.start()

    barrier = pltpu.get_barrier_semaphore()
    for k in range(1, NS):
        pl.semaphore_signal(
            barrier, inc=1, device_id=(lax.rem(me + k, NS), col), device_id_type=MESH
        )
    for c in (left, right):
        pl.semaphore_signal(barrier, inc=1, device_id=(me, c), device_id_type=MESH)
    pl.semaphore_wait(barrier, NS + 1)

    lanes = iota((1, W), 1)
    for s in range(NS):
        sketch_load(s).wait()
        kept = (lanes < ranks_ref[s]).astype(BF16)
        sk[s] = sk[s] * kept
    r_raw[me] = sk[me]

    def r_copy(k):
        s = lax.rem(me + k, NS)
        return pltpu.make_async_remote_copy(
            src_ref=sk.at[s], dst_ref=r_raw.at[me], send_sem=r_send.at[k - 1],
            recv_sem=r_recv.at[me], device_id=(s, col), device_id_type=MESH,
        )

    def r_arrival(r):
        return pltpu.make_async_remote_copy(
            src_ref=sk.at[0], dst_ref=r_raw.at[r], send_sem=r_send.at[0],
            recv_sem=r_recv.at[r], device_id=(me, col), device_id_type=MESH,
        )

    def w_copy(k):
        s = lax.rem(me + k, NS)
        return pltpu.make_async_remote_copy(
            src_ref=comp.at[me], dst_ref=comp.at[me], send_sem=w_send.at[k - 1],
            recv_sem=w_recv.at[me], device_id=(s, col), device_id_type=MESH,
        )

    def w_arrival(r):
        return pltpu.make_async_remote_copy(
            src_ref=comp.at[r], dst_ref=comp.at[r], send_sem=w_send.at[0],
            recv_sem=w_recv.at[r], device_id=(me, col), device_id_type=MESH,
        )

    def l_copy(r):
        return pltpu.make_async_remote_copy(
            src_ref=r_raw.at[r], dst_ref=l_raw.at[r], send_sem=l_send.at[r],
            recv_sem=l_recv.at[r], device_id=(me, right), device_id_type=MESH,
        )

    def gl_copy(r):
        return pltpu.make_async_remote_copy(
            src_ref=gl_out.at[r], dst_ref=gl_in.at[r], send_sem=gl_send.at[r],
            recv_sem=gl_recv.at[r], device_id=(me, right), device_id_type=MESH,
        )

    def gr_copy(r):
        return pltpu.make_async_remote_copy(
            src_ref=gr_out.at[r], dst_ref=gr_in.at[r], send_sem=gr_send.at[r],
            recv_sem=gr_recv.at[r], device_id=(me, left), device_id_type=MESH,
        )

    def o_copy(r):
        return pltpu.make_async_remote_copy(
            src_ref=bm.at[r + 1], dst_ref=out_ref.at[me], send_sem=o_send.at[r],
            recv_sem=o_recv.at[me], device_id=(r, col), device_id_type=MESH,
        )

    def o_arrival(s):
        return pltpu.make_async_remote_copy(
            src_ref=bm.at[1], dst_ref=out_ref.at[s], send_sem=o_send.at[0],
            recv_sem=o_recv.at[s], device_id=(me, col), device_id_type=MESH,
        )

    def o_stay(r):
        return pltpu.make_async_copy(bm.at[r + 1], out_ref.at[me], o_local)

    @pl.when(me == 0)
    def _():
        for k in (2, 1, 3):
            r_copy(k).start()

    compact_tensor(peps_ref, charges_ref, comp32)
    comp[me] = comp32[...].astype(BF16)
    for k in range(1, NS):
        w_copy(k).start()

    size = sizes_ref[me]
    boundary_load.wait()
    start = jnp.where(
        ((iota((W * D, W), 0) >> 3) < size) & (iota((W * D, W), 1) < size),
        bm[0].astype(F32), 0.0,
    )
    bm[0] = start.astype(BF16)
    tall[...] = start
    for u in range(D):
        mid[:, u * W : (u + 1) * W] = tall[pl.ds(u, W, stride=D), :].T
    for u in range(D):
        tall[pl.ds(u, W, stride=D), :] = mid[:, u * W : (u + 1) * W]
    bt[...] = tall[...].astype(BF16)

    block = iota((256, 256), 0) >> 6 == iota((256, 256), 1) >> 6

    def prepare_right(r):
        @pl.when(r != me)
        def _():
            r_arrival(r).wait_recv()

        l_copy(r).start()

        @pl.when((r == 0) & (me != 0))
        def _():
            for k in (2, 1, 3):
                r_copy(k).start()

        tall[...] = r_raw[r].astype(F32)
        for h in range(D):
            r_wide[:, h * W : (h + 1) * W] = tall[pl.ds(h, W, stride=D), :].astype(BF16)

        @pl.when(r != me)
        def _():
            w_arrival(r).wait_recv()

        for i in range(2):
            one = comp[r, i]
            kron[i] = jnp.where(block, jnp.concatenate([one] * 4, axis=0).astype(F32), 0.0).astype(
                BF16
            )

    def prepare_left(r):
        l_copy(r).wait_recv()
        natural = l_raw[r].astype(F32)
        tall[...] = natural
        for h in range(D):
            l_wide[:, h * W : (h + 1) * W] = tall[pl.ds(h, W, stride=D), :].astype(BF16)
        l_turned[...] = natural.T.astype(BF16)

    def sided(lhs, wide, tensor):
        part = mm(lhs, wide)
        columns = []
        for q in range(W // 4):
            pieces = [
                part[(4 * q + i) * D : (4 * q + i + 1) * D, h * W : (h + 1) * W]
                for i in range(4)
                for h in range(D)
            ]
            columns.append(jnp.concatenate(pieces, axis=0).astype(BF16))
        return mm(tensor, jnp.concatenate(columns, axis=1))

    prepare_right(0)

    def absorb(r, carry):
        side = sided(bm[r], r_wide[...], kron[0])
        for d in range(D):
            pieces = [
                side[(i * D + d) * D : (i * D + d + 1) * D, q * W : (q + 1) * W]
                for q in range(W // 4)
                for i in range(4)
            ]
            z[:, d * W : (d + 1) * W] = jnp.concatenate(pieces, axis=0).astype(BF16)
        gram = jnp.zeros((W, W), F32)
        for d in range(D):
            piece = z[:, d * W : (d + 1) * W]
            gram += mm_tn(piece, piece)
        gram_own[0] = gram
        gl_out[r] = gram.astype(BF16)
        gl_copy(r).start()

        @pl.when(r == 0)
        def _():
            prepare_left(0)

        side = sided(bt[...], l_wide[...], kron[1]).astype(BF16)
        for q in range(W // 4):
            z2[pl.ds(q * 256, 256), :] = side[:, q * W : (q + 1) * W]
        gram = mm_tn(z2[...], z2[...])
        gram_own[1] = gram
        gr_out[r] = gram.astype(BF16)
        gr_copy(r).start()
        mid[...] = mm(l_turned[...], z[...])

        @pl.when(r < NS - 1)
        def _():
            prepare_right(r + 1)
            prepare_left(r + 1)

        eye = (iota((W, W), 0) == iota((W, W), 1)).astype(F32)
        gl_copy(r).wait_recv()
        gr_copy(r).wait_recv()
        work[0, :, :W] = gl_in[r].astype(F32) + gram_own[1] + eye
        work[1, :, :W] = gr_in[r].astype(F32) + gram_own[0] + eye
        work[0, :, W:] = eye
        work[1, :, W:] = eye
        inverse_factors(work, inverse, mixed)
        lefted = mm3(inverse[0], mid[...])
        for d in range(D):
            tall[pl.ds(d, W, stride=D), :] = lefted[:, d * W : (d + 1) * W]
        high, low = halves(inverse[1])
        second = jnp.concatenate([high, low, high], axis=1)
        high, low = halves(tall[...])
        fresh = mm_nt(jnp.concatenate([high, high, low], axis=1), second)
        scaling = lax.rsqrt(jnp.mean(fresh * fresh) + 1e-6)
        bm[r + 1] = (fresh * scaling).astype(BF16)

        @pl.when(r != me)
        def _():
            o_copy(r).start()

        @pl.when(r == me)
        def _():
            o_stay(r).start()

        @pl.when(r < NS - 1)
        def _():
            high, low = halves(lefted)
            for d in range(D):
                lanes_d = slice(d * W, (d + 1) * W)
                piece = jnp.concatenate([high[:, lanes_d], high[:, lanes_d], low[:, lanes_d]], axis=1)
                tall[pl.ds(d, W, stride=D), :] = mm_nt(second, piece)
            bt[...] = (tall[...] * scaling).astype(BF16)

        return carry

    lax.fori_loop(0, NS, absorb, 0)

    for k in range(1, NS):
        r_copy(k).wait_send()
        w_copy(k).wait_send()
    for r in range(NS):
        l_copy(r).wait_send()
        gl_copy(r).wait_send()
        gr_copy(r).wait_send()
    for r in range(NS):

        @pl.when(r != me)
        def _():
            o_copy(r).wait_send()
            o_arrival(r).wait_recv()

    o_stay(me).wait()


def body(boundary, peps_rows, sketch, ranks, sizes, charges):
    any_space = pl.BlockSpec(memory_space=pl.ANY)
    smem = pl.BlockSpec(memory_space=pltpu.SMEM)
    vmem = pl.BlockSpec(memory_space=pltpu.VMEM)
    dma = pltpu.SemaphoreType.DMA
    result = pl.pallas_call(
        kernel,
        out_shape=jax.ShapeDtypeStruct((NS, W * D, W), BF16),
        in_specs=[vmem, smem, smem, smem, any_space, any_space],
        out_specs=any_space,
        scratch_shapes=[
            pltpu.VMEM((NS, W * D, W), BF16),
            pltpu.VMEM((NS + 1, W * D, W), BF16),
            pltpu.VMEM((W * D, W), BF16),
            pltpu.VMEM((NS, W * D, W), BF16),
            pltpu.VMEM((NS, W * D, W), BF16),
            pltpu.VMEM((W, W * D), BF16),
            pltpu.VMEM((W, W * D), BF16),
            pltpu.VMEM((W, W * D), BF16),
            pltpu.VMEM((2, 64, 256), F32),
            pltpu.VMEM((NS, 2, 64, 256), BF16),
            pltpu.VMEM((2, 256, 256), BF16),
            pltpu.VMEM((W * D, W * D), BF16),
            pltpu.VMEM((W // 4 * 256, W), BF16),
            pltpu.VMEM((W, W * D), F32),
            pltpu.VMEM((W * D, W), F32),
            pltpu.VMEM((2, W, W), F32),
            pltpu.VMEM((NS, W, W), BF16),
            pltpu.VMEM((NS, W, W), BF16),
            pltpu.VMEM((NS, W, W), BF16),
            pltpu.VMEM((NS, W, W), BF16),
            pltpu.VMEM((2, W, 2 * W), F32),
            pltpu.VMEM((2, W, W), F32),
            pltpu.VMEM((W, 4 * W), F32),
            dma((NS,)), dma(()), dma((NS - 1,)), dma((NS,)), dma((NS - 1,)), dma((NS,)),
            dma((NS,)), dma((NS,)), dma((NS,)), dma((NS,)), dma((NS,)), dma((NS,)),
            dma((NS,)), dma((NS,)), dma(()),
        ],
        compiler_params=pltpu.CompilerParams(
            collective_id=0, has_side_effects=True, vmem_limit_bytes=56 * 2**20
        ),
        name="absorb_rows",
    )(
        peps_rows.reshape(D * D, D, D),
        ranks.reshape(NS),
        sizes,
        charges,
        boundary.reshape(NS, W * D, W),
        sketch.reshape(NS, W * D, W),
    )
    return result.reshape(1, 1, NS, W, D, W)


def solution(mesh):
    placed = (
        P("col", None, None, None, None),
        P("row", "col", None, None, None, None),
        P("row", "col", None, None, None),
        P("row", "col", None),
        P(),
        P(),
    )
    return jax.shard_map(
        body,
        mesh=mesh,
        in_specs=placed,
        out_specs=P("row", "col", None, None, None, None),
        check_vma=False,
    )
```

```python
import jax
import jax.numpy as jnp
from jax import lax
from jax.experimental import pallas as pl
from jax.experimental.pallas import tpu as pltpu
from jax.sharding import PartitionSpec as P

W = 128
D = 8
NS = 4
CHUNKS = 4
CHUNK = W * D // CHUNKS
F32 = jnp.float32
BF16 = jnp.bfloat16
MESH = pl.DeviceIdType.MESH


def iota(shape, axis):
    return lax.broadcasted_iota(jnp.int32, shape, axis)


def mm(a, b):
    return jnp.dot(a, b, preferred_element_type=F32)


def mm_nt(a, b):
    return lax.dot_general(a, b, (((1,), (1,)), ((), ())), preferred_element_type=F32)


def mm_tn(a, b):
    return lax.dot_general(a, b, (((0,), (0,)), ((), ())), preferred_element_type=F32)


def compact_tensor(peps_ref, charges_ref, compact):
    rows = iota((512, 1), 0)
    l, h, u = rows >> 6, (rows >> 3) & 7, rows & 7
    balance = jnp.zeros((512, 1), jnp.int32)
    for i in range(D):
        q = charges_ref[i]
        balance += q * (
            (l == i).astype(jnp.int32) + (u == i).astype(jnp.int32) - (h == i).astype(jnp.int32)
        )
    values = peps_ref[...].astype(F32).reshape(512, D)
    big = iota((512, W), 0)
    lane = iota((512, W), 1)
    from_row = jnp.where(lane < 64, big & 63, ((big >> 6) << 3) | (big & 7))
    same = from_row == (lane & 63)
    pick = iota((2 * D, 512), 0)
    source = iota((2 * D, 512), 1)
    wanted = jnp.where(pick < D, source >> 6, (source >> 3) & 7)
    picker = (wanted == (pick & 7)).astype(BF16)
    for d in range(D):
        column = jnp.where(balance == charges_ref[d], values[:, d : d + 1], 0.0)
        spread = jnp.where(same, jnp.broadcast_to(column, (512, W)), 0.0).astype(BF16)
        both = mm(picker, spread)
        compact[pl.ds(d * D, D), :] = jnp.where(iota((D, W), 1) < 64, both[:D], both[D:])


def halves(x):
    high = x.astype(BF16)
    return high, (x - high.astype(F32)).astype(BF16)


def mm3(a, b):
    ah, al = halves(a)
    bh, bl = halves(b)
    return mm(jnp.concatenate([ah, ah, al], axis=1), jnp.concatenate([bh, bl, bh], axis=0))


def mm3_tn(a, b):
    ah, al = halves(a)
    bh, bl = halves(b)
    return mm_tn(jnp.concatenate([ah, ah, al], axis=0), jnp.concatenate([bh, bl, bh], axis=0))


def vreg(x):
    return jnp.broadcast_to(x, (8, W))


def eliminate(tiles, first, part):
    sub = iota((8, W), 0)
    tiles = list(tiles)

    def spread(v, j):
        a, b = (first[0] + j) % W, (first[1] + j) % W
        return jnp.where(part, vreg(v[:, a : a + 1]), vreg(v[:, b : b + 1]))

    for q in range(4):
        columns = [spread(tiles[q], 8 * q + t) for t in range(8)]
        s = {(i, t): vreg(columns[t][i : i + 1, :]) for t in range(8) for i in range(t, 8)}
        low = {o: [spread(tiles[o], 8 * q + t) for t in range(8)] for o in range(q + 1, 4)}
        f, n, root = {}, {}, []
        for t in range(8):
            root.append(lax.rsqrt(s[t, t]))
            over = root[t] * root[t]
            for i in range(t + 1, 8):
                f[i, t] = s[i, t] * over
                for k in range(t + 1, i + 1):
                    s[i, k] = s[i, k] - (s[i, t] * s[k, t]) * over
        for j in range(8):
            for i in range(j + 1, 8):
                total = f[i, j]
                for k in range(j + 1, i):
                    total = total + f[i, k] * n[k, j]
                n[i, j] = -total
        g = {
            (i, j): (root[i] if i == j else n[i, j] * root[i])
            for j in range(8)
            for i in range(j, 8)
        }
        panel, result = tiles[q], None
        for j in range(8):
            column = jnp.zeros((8, W), F32)
            for i in range(j, 8):
                column = jnp.where(sub == i, g[i, j], column)
            term = column * vreg(panel[j : j + 1, :])
            result = term if result is None else result + term
        tiles[q] = result
        for o in range(q + 1, 4):
            rest = tiles[o]
            for t in range(8):
                factor = None
                for j in range(t + 1):
                    term = low[o][j] * g[t, j]
                    factor = term if factor is None else factor + term
                rest = rest - factor * vreg(result[t : t + 1, :])
            tiles[o] = rest
    return tiles


def inverse_factors(work, inverse, mixed):
    lane, sub = iota((8, W), 1), iota((8, W), 0)
    group = lane >> 5
    for k in range(4):
        at = [(k + i) % 4 for i in range(4)]
        part = (group == at[0]) | (group == at[1])
        tiles = []
        for q in range(4):
            rows = pl.ds(32 * k + 8 * q, 8)
            one = work[0, rows, :W]
            two = pltpu.roll(work[1, rows, :W], 64, 1)
            unit = ((lane & 31) == (sub + 8 * q)).astype(F32)
            tiles.append(jnp.where(group == at[0], one, jnp.where(group == at[2], two, unit)))
        done = jnp.concatenate(eliminate(tiles, (32 * k, 32 * k + 64), part), axis=0)
        mixed[...] = jnp.zeros((W, 4 * W), F32)
        mixed[pl.ds(32 * at[1], 32), : 2 * W] = work[0, pl.ds(32 * k, 32), :]
        mixed[pl.ds(32 * at[3], 32), 2 * W :] = work[1, pl.ds(32 * k, 32), :]
        both = mm3(done, mixed[...])
        for i in range(2):
            panel = both[:, i * 2 * W : (i + 1) * 2 * W]
            inverse[i, pl.ds(32 * k, 32), :] = panel[:, W:]
            if k < 3:
                below = 32 * (k + 1)
                update = mm3_tn(panel[:, :W], panel)
                work[i, pl.ds(below, W - below), :] -= update[below:, :]


def kernel(
    peps_ref, ranks_ref, sizes_ref, charges_ref, boundary_ref, sketch_ref, out_ref,
    sk, bm, sides, r_raw, l_raw, wides, l_turned, comp32, comp, kron, z, mid, tall,
    gram_own, gram_out, gram_in, work, inverse, mixed,
    sk_sem, b_sem, r_send, r_recv, w_send, w_recv, l_send, l_recv,
    g_send, g_recv, o_send, o_recv, o_local,
):
    me = lax.axis_index("row")
    col = lax.axis_index("col")
    cols = lax.axis_size("col")
    right = lax.rem(col + 1, cols)
    left = lax.rem(col + cols - 1, cols)

    def sketch_load(s):
        return pltpu.make_async_copy(sketch_ref.at[s], sk.at[s], sk_sem.at[s])

    def chunk(c):
        return pl.ds(c * CHUNK, CHUNK)

    def r_copy(k, c):
        s = lax.rem(me + k, NS)
        return pltpu.make_async_remote_copy(
            src_ref=sk.at[s, chunk(c)], dst_ref=r_raw.at[me, chunk(c)],
            send_sem=r_send.at[k - 1, c], recv_sem=r_recv.at[me, c],
            device_id=(s, col), device_id_type=MESH,
        )

    def r_arrival(r, c):
        return pltpu.make_async_remote_copy(
            src_ref=sk.at[0, chunk(c)], dst_ref=r_raw.at[r, chunk(c)],
            send_sem=r_send.at[0, c], recv_sem=r_recv.at[r, c],
            device_id=(me, col), device_id_type=MESH,
        )

    def l_copy(r, c):
        return pltpu.make_async_remote_copy(
            src_ref=r_raw.at[r, chunk(c)], dst_ref=l_raw.at[r, chunk(c)],
            send_sem=l_send.at[r, c], recv_sem=l_recv.at[r, c],
            device_id=(me, right), device_id_type=MESH,
        )

    def w_copy(k):
        s = lax.rem(me + k, NS)
        return pltpu.make_async_remote_copy(
            src_ref=comp.at[me], dst_ref=comp.at[me], send_sem=w_send.at[k - 1],
            recv_sem=w_recv.at[me], device_id=(s, col), device_id_type=MESH,
        )

    def w_arrival(r):
        return pltpu.make_async_remote_copy(
            src_ref=comp.at[r], dst_ref=comp.at[r], send_sem=w_send.at[0],
            recv_sem=w_recv.at[r], device_id=(me, col), device_id_type=MESH,
        )

    def g_copy(r, side):
        return pltpu.make_async_remote_copy(
            src_ref=gram_out.at[r, side], dst_ref=gram_in.at[r, side],
            send_sem=g_send.at[r, side], recv_sem=g_recv.at[r, side],
            device_id=(me, right + side * (left - right)), device_id_type=MESH,
        )

    def o_copy(r):
        return pltpu.make_async_remote_copy(
            src_ref=bm.at[r + 1], dst_ref=out_ref.at[me], send_sem=o_send.at[r],
            recv_sem=o_recv.at[me], device_id=(r, col), device_id_type=MESH,
        )

    def o_arrival(s):
        return pltpu.make_async_remote_copy(
            src_ref=bm.at[1], dst_ref=out_ref.at[s], send_sem=o_send.at[0],
            recv_sem=o_recv.at[s], device_id=(me, col), device_id_type=MESH,
        )

    def o_stay(r):
        return pltpu.make_async_copy(bm.at[r + 1], out_ref.at[me], o_local)

    def send_sketch(k):
        for c in range(CHUNKS):
            r_copy(k, c).start()

    barrier = pltpu.get_barrier_semaphore()
    for k in range(1, NS):
        pl.semaphore_signal(
            barrier, inc=1, device_id=(lax.rem(me + k, NS), col), device_id_type=MESH
        )
    for c in (left, right):
        pl.semaphore_signal(barrier, inc=1, device_id=(me, c), device_id_type=MESH)
    for s in range(NS):
        sketch_load(s).start()
    boundary_load = pltpu.make_async_copy(boundary_ref.at[me], bm.at[0], b_sem)
    boundary_load.start()
    lanes = iota((1, W), 1)
    for s in range(NS):
        sketch_load(s).wait()
        sk[s] = sk[s] * (lanes < ranks_ref[s]).astype(BF16)
    r_raw[me] = sk[me]
    pl.semaphore_wait(barrier, NS + 1)

    @pl.when(me == 0)
    def _():
        send_sketch(1)
        send_sketch(3)

    @pl.when(me == 1)
    def _():
        send_sketch(3)

    @pl.when(me == 2)
    def _():
        send_sketch(1)
        send_sketch(3)
        send_sketch(2)

    compact_tensor(peps_ref, charges_ref, comp32)
    comp[me] = comp32[...].astype(BF16)
    for k in range(1, NS):
        w_copy(k).start()

    block = iota((256, 256), 0) >> 6 == iota((256, 256), 1) >> 6

    def relay(r):
        for c in range(CHUNKS):

            @pl.when(r != me)
            def _():
                r_arrival(r, c).wait_recv()

            l_copy(r, c).start()

        @pl.when(r != me)
        def _():
            w_arrival(r).wait_recv()

    def regroup(side, natural):
        tall[...] = natural
        for h in range(D):
            wides[side, :, h * W : (h + 1) * W] = tall[pl.ds(h, W, stride=D), :].astype(BF16)

    def prepare_right(r):
        regroup(0, r_raw[r].astype(F32))
        both = comp[r].astype(F32)
        turned = pltpu.roll(both, 64, 1)
        low = iota((64, W), 1) < 64
        for i, (one, two) in enumerate(((both, turned), (turned, both))):
            twice = jnp.where(low, one, two)
            four = jnp.concatenate([twice, twice], axis=1)
            kron[i] = jnp.where(block, jnp.concatenate([four] * 4, axis=0), 0.0).astype(BF16)

    def prepare_left(r):
        natural = l_raw[r].astype(F32)
        regroup(1, natural)
        l_turned[...] = natural.T.astype(BF16)

    def left_arrives(r):
        for c in range(CHUNKS):
            l_copy(r, c).wait_recv()

    def absorb_side(r, side):
        part = mm(sides[side], wides[side])
        columns = []
        for q in range(W // 4):
            pieces = [
                part[(4 * q + i) * D : (4 * q + i + 1) * D, h * W : (h + 1) * W]
                for i in range(4)
                for h in range(D)
            ]
            columns.append(jnp.concatenate(pieces, axis=0).astype(BF16))
        whole = mm(kron[side], jnp.concatenate(columns, axis=1))
        for d in range(D):
            pieces = [
                whole[(i * D + d) * D : (i * D + d + 1) * D, q * W : (q + 1) * W]
                for q in range(W // 4)
                for i in range(4)
            ]
            z[side, :, d * W : (d + 1) * W] = jnp.concatenate(pieces, axis=0).astype(BF16)
        gram = jnp.zeros((W, W), F32)
        for d in range(D):
            piece = z[side, :, d * W : (d + 1) * W]
            gram += mm_tn(piece, piece)
        gram_own[side] = gram
        gram_out[r, side] = gram.astype(BF16)
        g_copy(r, side).start()

    @pl.when(me == 0)
    def _():
        for c in range(CHUNKS):
            r_copy(1, c).wait_send()
        send_sketch(2)

    size = sizes_ref[me]
    boundary_load.wait()
    start = jnp.where(
        ((iota((W * D, W), 0) >> 3) < size) & (iota((W * D, W), 1) < size),
        bm[0].astype(F32), 0.0,
    )
    sides[0] = start.astype(BF16)
    tall[...] = start
    for u in range(D):
        mid[:, u * W : (u + 1) * W] = tall[pl.ds(u, W, stride=D), :].T
    for u in range(D):
        tall[pl.ds(u, W, stride=D), :] = mid[:, u * W : (u + 1) * W]
    sides[1] = tall[...].astype(BF16)

    relay(0)
    prepare_right(0)
    eye = (iota((W, W), 0) == iota((W, W), 1)).astype(F32)

    def absorb(r, carry):
        early = jnp.where(r == 0, 0, 1 - lax.rem(col, 2))
        absorb_side(r, early)

        @pl.when(r == 0)
        def _():
            left_arrives(0)

            @pl.when(me == 1)
            def _():
                send_sketch(1)

            prepare_left(0)

        absorb_side(r, 1 - early)
        mid[...] = mm(l_turned[...], z[0])

        @pl.when((r == 0) & (me == 1))
        def _():
            send_sketch(2)

        @pl.when((r == 0) & (me == 3))
        def _():
            for k in range(1, NS):
                send_sketch(k)

        @pl.when(r < NS - 1)
        def _():
            relay(r + 1)

        for side in range(2):
            g_copy(r, side).wait_recv()
        for side in range(2):
            work[side, :, :W] = gram_in[r, side].astype(F32) + gram_own[1 - side] + eye
            work[side, :, W:] = eye
        prepare_right(jnp.minimum(r + 1, NS - 1))
        inverse_factors(work, inverse, mixed)

        @pl.when(r < NS - 1)
        def _():
            left_arrives(r + 1)
            prepare_left(r + 1)

        lefted = mm3(inverse[0], mid[...])
        for d in range(D):
            tall[pl.ds(d, W, stride=D), :] = lefted[:, d * W : (d + 1) * W]
        high, low = halves(inverse[1])
        second = jnp.concatenate([high, low, high], axis=1)
        high, low = halves(tall[...])
        fresh = mm_nt(jnp.concatenate([high, high, low], axis=1), second)
        scaling = lax.rsqrt(jnp.mean(fresh * fresh) + 1e-6)
        result = (fresh * scaling).astype(BF16)
        bm[r + 1] = result

        @pl.when(r != me)
        def _():
            o_copy(r).start()

        @pl.when(r == me)
        def _():
            o_stay(r).start()

        @pl.when(r < NS - 1)
        def _():
            sides[0] = result
            high, low = halves(lefted)
            for d in range(D):
                lanes_d = slice(d * W, (d + 1) * W)
                piece = jnp.concatenate([high[:, lanes_d], high[:, lanes_d], low[:, lanes_d]], axis=1)
                tall[pl.ds(d, W, stride=D), :] = mm_nt(second, piece)
            sides[1] = (tall[...] * scaling).astype(BF16)

        return carry

    lax.fori_loop(0, NS, absorb, 0)

    for c in range(CHUNKS):

        @pl.when(me != 0)
        def _():
            r_copy(1, c).wait_send()

        r_copy(2, c).wait_send()
        r_copy(3, c).wait_send()
        for r in range(NS):
            l_copy(r, c).wait_send()
    for k in range(1, NS):
        w_copy(k).wait_send()
    for r in range(NS):
        for side in range(2):
            g_copy(r, side).wait_send()

        @pl.when(r != me)
        def _():
            o_copy(r).wait_send()
            o_arrival(r).wait_recv()

    o_stay(me).wait()


def body(boundary, peps_rows, sketch, ranks, sizes, charges):
    any_space = pl.BlockSpec(memory_space=pl.ANY)
    smem = pl.BlockSpec(memory_space=pltpu.SMEM)
    vmem = pl.BlockSpec(memory_space=pltpu.VMEM)
    dma = pltpu.SemaphoreType.DMA
    result = pl.pallas_call(
        kernel,
        out_shape=jax.ShapeDtypeStruct((NS, W * D, W), BF16),
        in_specs=[vmem, smem, smem, smem, any_space, any_space],
        out_specs=any_space,
        scratch_shapes=[
            pltpu.VMEM((NS, W * D, W), BF16),
            pltpu.VMEM((NS + 1, W * D, W), BF16),
            pltpu.VMEM((2, W * D, W), BF16),
            pltpu.VMEM((NS, W * D, W), BF16),
            pltpu.VMEM((NS, W * D, W), BF16),
            pltpu.VMEM((2, W, W * D), BF16),
            pltpu.VMEM((W, W * D), BF16),
            pltpu.VMEM((64, W), F32),
            pltpu.VMEM((NS, 64, W), BF16),
            pltpu.VMEM((2, 256, 256), BF16),
            pltpu.VMEM((2, W * D, W * D), BF16),
            pltpu.VMEM((W, W * D), F32),
            pltpu.VMEM((W * D, W), F32),
            pltpu.VMEM((2, W, W), F32),
            pltpu.VMEM((NS, 2, W, W), BF16),
            pltpu.VMEM((NS, 2, W, W), BF16),
            pltpu.VMEM((2, W, 2 * W), F32),
            pltpu.VMEM((2, W, W), F32),
            pltpu.VMEM((W, 4 * W), F32),
            dma((NS,)), dma(()), dma((NS - 1, CHUNKS)), dma((NS, CHUNKS)), dma((NS - 1,)),
            dma((NS,)), dma((NS, CHUNKS)), dma((NS, CHUNKS)), dma((NS, 2)), dma((NS, 2)),
            dma((NS,)), dma((NS,)), dma(()),
        ],
        compiler_params=pltpu.CompilerParams(
            collective_id=0, has_side_effects=True, vmem_limit_bytes=56 * 2**20
        ),
        name="absorb_rows",
    )(
        peps_rows.reshape(D * D, D, D),
        ranks.reshape(NS),
        sizes,
        charges,
        boundary.reshape(NS, W * D, W),
        sketch.reshape(NS, W * D, W),
    )
    return result.reshape(1, 1, NS, W, D, W)


def solution(mesh):
    placed = (
        P("col", None, None, None, None),
        P("row", "col", None, None, None, None),
        P("row", "col", None, None, None),
        P("row", "col", None),
        P(),
        P(),
    )
    return jax.shard_map(
        body,
        mesh=mesh,
        in_specs=placed,
        out_specs=P("row", "col", None, None, None, None),
        check_vma=False,
    )
```

```python
import jax
import jax.numpy as jnp
from jax import lax
from jax.experimental import pallas as pl
from jax.experimental.pallas import tpu as pltpu
from jax.sharding import PartitionSpec as P

W = 128
D = 8
NS = 4
CHUNKS = 4
HOPS = 2
CHUNK = W * D // CHUNKS
F32 = jnp.float32
BF16 = jnp.bfloat16
MESH = pl.DeviceIdType.MESH


def iota(shape, axis):
    return lax.broadcasted_iota(jnp.int32, shape, axis)


def mm(a, b):
    return jnp.dot(a, b, preferred_element_type=F32)


def mm_nt(a, b):
    return lax.dot_general(a, b, (((1,), (1,)), ((), ())), preferred_element_type=F32)


def mm_tn(a, b):
    return lax.dot_general(a, b, (((0,), (0,)), ((), ())), preferred_element_type=F32)


def compact_tensor(peps_ref, charges_ref, compact):
    rows = iota((512, 1), 0)
    l, h, u = rows >> 6, (rows >> 3) & 7, rows & 7
    balance = jnp.zeros((512, 1), jnp.int32)
    for i in range(D):
        q = charges_ref[i]
        balance += q * (
            (l == i).astype(jnp.int32) + (u == i).astype(jnp.int32) - (h == i).astype(jnp.int32)
        )
    values = peps_ref[...].astype(F32).reshape(512, D)
    big = iota((512, W), 0)
    lane = iota((512, W), 1)
    from_row = jnp.where(lane < 64, big & 63, ((big >> 6) << 3) | (big & 7))
    same = from_row == (lane & 63)
    pick = iota((2 * D, 512), 0)
    source = iota((2 * D, 512), 1)
    wanted = jnp.where(pick < D, source >> 6, (source >> 3) & 7)
    picker = (wanted == (pick & 7)).astype(BF16)
    for d in range(D):
        column = jnp.where(balance == charges_ref[d], values[:, d : d + 1], 0.0)
        spread = jnp.where(same, jnp.broadcast_to(column, (512, W)), 0.0).astype(BF16)
        both = mm(picker, spread)
        compact[pl.ds(d * D, D), :] = jnp.where(iota((D, W), 1) < 64, both[:D], both[D:])


def halves(x):
    high = x.astype(BF16)
    return high, (x - high.astype(F32)).astype(BF16)


def mm3(a, b):
    ah, al = halves(a)
    bh, bl = halves(b)
    return mm(jnp.concatenate([ah, ah, al], axis=1), jnp.concatenate([bh, bl, bh], axis=0))


def mm3_tn(a, b):
    ah, al = halves(a)
    bh, bl = halves(b)
    return mm_tn(jnp.concatenate([ah, ah, al], axis=0), jnp.concatenate([bh, bl, bh], axis=0))


def vreg(x):
    return jnp.broadcast_to(x, (8, W))


def eliminate(tiles, first, part):
    sub = iota((8, W), 0)
    tiles = list(tiles)

    def spread(v, j):
        a, b = (first[0] + j) % W, (first[1] + j) % W
        return jnp.where(part, vreg(v[:, a : a + 1]), vreg(v[:, b : b + 1]))

    def row(x, i):
        return vreg(x[i : i + 1, :])

    own = [spread(tiles[0], t) for t in range(8)]
    for q in range(4):
        low = {o: [spread(tiles[o], 8 * q + t) for t in range(8)] for o in range(q + 1, 4)}
        after = [spread(tiles[q + 1], 8 * q + 8 + t) for t in range(8)] if q < 3 else []
        pivots = None
        for t in range(8):
            pivot = row(own[t], t)
            over = 1.0 / pivot
            pivots = pivot if t == 0 else jnp.where(sub == t, pivot, pivots)
            factor = jnp.where(sub > t, own[t] * over, 0.0)
            beside = {k: row(own[t], k) for k in range(t + 1, 8)}
            for k in range(t + 1, 8):
                own[k] = own[k] - factor * beside[k]
            here = row(tiles[q], t)
            for o in range(q + 1, 4):
                below = low[o][t] * over
                if o == q + 1:
                    for k in range(8):
                        after[k] = after[k] - below * row(low[o][t], k)
                for k in range(t + 1, 8):
                    low[o][k] = low[o][k] - below * beside[k]
                tiles[o] = tiles[o] - below * here
            if t < 7:
                tiles[q] = tiles[q] - factor * here
        tiles[q] = tiles[q] * lax.rsqrt(pivots)
        own = after
    return tiles


def inverse_factors(work, inverse, mixed):
    lane, sub = iota((8, W), 1), iota((8, W), 0)
    group = lane >> 5
    for k in range(4):
        at = [(k + i) % 4 for i in range(4)]
        part = (group == at[0]) | (group == at[1])
        tiles = []
        for q in range(4):
            rows = pl.ds(32 * k + 8 * q, 8)
            one = work[0, rows, :W]
            two = pltpu.roll(work[1, rows, :W], 64, 1)
            unit = ((lane & 31) == (sub + 8 * q)).astype(F32)
            tiles.append(jnp.where(group == at[0], one, jnp.where(group == at[2], two, unit)))
        done = jnp.concatenate(eliminate(tiles, (32 * k, 32 * k + 64), part), axis=0)
        mixed[...] = jnp.zeros((W, 4 * W), F32)
        mixed[pl.ds(32 * at[1], 32), : 2 * W] = work[0, pl.ds(32 * k, 32), :]
        mixed[pl.ds(32 * at[3], 32), 2 * W :] = work[1, pl.ds(32 * k, 32), :]
        both = mm3(done, mixed[...])
        for i in range(2):
            panel = both[:, i * 2 * W : (i + 1) * 2 * W]
            inverse[i, pl.ds(32 * k, 32), :] = panel[:, W:]
            if k < 3:
                below = 32 * (k + 1)
                update = mm3_tn(panel[:, :W], panel)
                work[i, pl.ds(below, W - below), :] -= update[below:, :]


def kernel(
    peps_ref, ranks_ref, sizes_ref, charges_ref, boundary_ref, sketch_ref, out_ref,
    sk, bm, sides, r_raw, l_raw, wides, l_turned, comp32, comp, kron, z, mid, tall,
    gram_own, gram_out, gram_in, work, inverse, mixed, hop,
    sk_sem, b_sem, r_send, r_recv, w_send, w_recv, l_send, l_recv,
    g_send, g_recv, o_send, o_recv, o_local, hop_recv, hop_send,
):
    me = lax.axis_index("row")
    col = lax.axis_index("col")
    cols = lax.axis_size("col")
    right = lax.rem(col + 1, cols)
    left = lax.rem(col + cols - 1, cols)

    def sketch_load(s):
        return pltpu.make_async_copy(sketch_ref.at[s], sk.at[s], sk_sem.at[s])

    def chunk(c):
        return pl.ds(c * CHUNK, CHUNK)

    def r_copy(k, c):
        s = lax.rem(me + k, NS)
        return pltpu.make_async_remote_copy(
            src_ref=sk.at[s, chunk(c)], dst_ref=r_raw.at[me, chunk(c)],
            send_sem=r_send.at[k - 1, c], recv_sem=r_recv.at[me, c],
            device_id=(s, col), device_id_type=MESH,
        )

    def r_arrival(r, c):
        return pltpu.make_async_remote_copy(
            src_ref=sk.at[0, chunk(c)], dst_ref=r_raw.at[r, chunk(c)],
            send_sem=r_send.at[0, c], recv_sem=r_recv.at[r, c],
            device_id=(me, col), device_id_type=MESH,
        )

    def l_copy(r, c):
        return pltpu.make_async_remote_copy(
            src_ref=r_raw.at[r, chunk(c)], dst_ref=l_raw.at[r, chunk(c)],
            send_sem=l_send.at[r, c], recv_sem=l_recv.at[r, c],
            device_id=(me, right), device_id_type=MESH,
        )

    def w_copy(k):
        s = lax.rem(me + k, NS)
        return pltpu.make_async_remote_copy(
            src_ref=comp.at[me], dst_ref=comp.at[me], send_sem=w_send.at[k - 1],
            recv_sem=w_recv.at[me], device_id=(s, col), device_id_type=MESH,
        )

    def w_arrival(r):
        return pltpu.make_async_remote_copy(
            src_ref=comp.at[r], dst_ref=comp.at[r], send_sem=w_send.at[0],
            recv_sem=w_recv.at[r], device_id=(me, col), device_id_type=MESH,
        )

    def g_copy(r, side):
        return pltpu.make_async_remote_copy(
            src_ref=gram_out.at[r, side], dst_ref=gram_in.at[r, side],
            send_sem=g_send.at[r, side], recv_sem=g_recv.at[r, side],
            device_id=(me, right + side * (left - right)), device_id_type=MESH,
        )

    def o_copy(r):
        return pltpu.make_async_remote_copy(
            src_ref=bm.at[r + 1], dst_ref=out_ref.at[me], send_sem=o_send.at[r],
            recv_sem=o_recv.at[me], device_id=(r, col), device_id_type=MESH,
        )

    def o_arrival(s):
        return pltpu.make_async_remote_copy(
            src_ref=bm.at[1], dst_ref=out_ref.at[s], send_sem=o_send.at[0],
            recv_sem=o_recv.at[s], device_id=(me, col), device_id_type=MESH,
        )

    def o_stay(r):
        return pltpu.make_async_copy(bm.at[r + 1], out_ref.at[me], o_local)

    def hop_in(c):
        return pltpu.make_async_remote_copy(
            src_ref=sk.at[2, chunk(c)], dst_ref=hop.at[c], send_sem=r_send.at[1, c],
            recv_sem=hop_recv.at[c], device_id=(3, col), device_id_type=MESH,
        )

    def hop_on(c):
        return pltpu.make_async_remote_copy(
            src_ref=hop.at[c], dst_ref=r_raw.at[0, chunk(c)], send_sem=hop_send.at[c],
            recv_sem=r_recv.at[0, c], device_id=(2, col), device_id_type=MESH,
        )

    def send_sketch(k):
        for c in range(CHUNKS):
            r_copy(k, c).start()

    barrier = pltpu.get_barrier_semaphore()
    for k in range(1, NS):
        pl.semaphore_signal(
            barrier, inc=1, device_id=(lax.rem(me + k, NS), col), device_id_type=MESH
        )
    for c in (left, right):
        pl.semaphore_signal(barrier, inc=1, device_id=(me, c), device_id_type=MESH)
    for s in range(NS):
        sketch_load(s).start()
    boundary_load = pltpu.make_async_copy(boundary_ref.at[me], bm.at[0], b_sem)
    boundary_load.start()
    lanes = iota((1, W), 1)
    for s in range(NS):
        sketch_load(s).wait()
        sk[s] = sk[s] * (lanes < ranks_ref[s]).astype(BF16)
    r_raw[me] = sk[me]
    pl.semaphore_wait(barrier, NS + 1)

    @pl.when(me == 0)
    def _():
        send_sketch(1)
        for c in range(HOPS):
            hop_in(c).start()

    @pl.when(me == 1)
    def _():
        send_sketch(3)

    @pl.when(me == 2)
    def _():
        send_sketch(1)
        send_sketch(3)
        send_sketch(2)

    compact_tensor(peps_ref, charges_ref, comp32)
    comp[me] = comp32[...].astype(BF16)
    for k in range(1, NS):
        w_copy(k).start()

    block = iota((256, 256), 0) >> 6 == iota((256, 256), 1) >> 6

    def relay(r):
        for c in range(CHUNKS):

            @pl.when(r != me)
            def _():
                r_arrival(r, c).wait_recv()

            l_copy(r, c).start()

        @pl.when(r != me)
        def _():
            w_arrival(r).wait_recv()

    def regroup(side, natural):
        tall[...] = natural
        for h in range(D):
            wides[side, :, h * W : (h + 1) * W] = tall[pl.ds(h, W, stride=D), :].astype(BF16)

    def prepare_right(r):
        regroup(0, r_raw[r].astype(F32))
        both = comp[r].astype(F32)
        turned = pltpu.roll(both, 64, 1)
        low = iota((64, W), 1) < 64
        for i, (one, two) in enumerate(((both, turned), (turned, both))):
            twice = jnp.where(low, one, two)
            four = jnp.concatenate([twice, twice], axis=1)
            kron[i] = jnp.where(block, jnp.concatenate([four] * 4, axis=0), 0.0).astype(BF16)

    def prepare_left(r):
        natural = l_raw[r].astype(F32)
        regroup(1, natural)
        l_turned[...] = natural.T.astype(BF16)

    def left_arrives(r):
        for c in range(CHUNKS):
            l_copy(r, c).wait_recv()

    def absorb_side(r, side):
        part = mm(sides[side], wides[side])
        columns = []
        for q in range(W // 4):
            pieces = [
                part[(4 * q + i) * D : (4 * q + i + 1) * D, h * W : (h + 1) * W]
                for i in range(4)
                for h in range(D)
            ]
            columns.append(jnp.concatenate(pieces, axis=0).astype(BF16))
        whole = mm(kron[side], jnp.concatenate(columns, axis=1))
        for d in range(D):
            pieces = [
                whole[(i * D + d) * D : (i * D + d + 1) * D, q * W : (q + 1) * W]
                for q in range(W // 4)
                for i in range(4)
            ]
            z[side, :, d * W : (d + 1) * W] = jnp.concatenate(pieces, axis=0).astype(BF16)
        gram = jnp.zeros((W, W), F32)
        for d in range(D):
            piece = z[side, :, d * W : (d + 1) * W]
            gram += mm_tn(piece, piece)
        gram_own[side] = gram
        gram_out[r, side] = gram.astype(BF16)
        g_copy(r, side).start()

    size = sizes_ref[me]
    boundary_load.wait()
    start = jnp.where(
        ((iota((W * D, W), 0) >> 3) < size) & (iota((W * D, W), 1) < size),
        bm[0].astype(F32), 0.0,
    )
    sides[0] = start.astype(BF16)
    tall[...] = start
    for u in range(D):
        mid[:, u * W : (u + 1) * W] = tall[pl.ds(u, W, stride=D), :].T
    for u in range(D):
        tall[pl.ds(u, W, stride=D), :] = mid[:, u * W : (u + 1) * W]
    sides[1] = tall[...].astype(BF16)

    @pl.when(me == 3)
    def _():
        for c in range(HOPS):
            hop_in(c).wait_recv()
            hop_on(c).start()

    relay(0)
    prepare_right(0)

    eye = (iota((W, W), 0) == iota((W, W), 1)).astype(F32)

    def absorb(r, carry):
        early = jnp.where(r == 0, 0, 1 - lax.rem(col, 2))
        absorb_side(r, early)

        @pl.when(r == 0)
        def _():
            @pl.when(me == 0)
            def _():
                for c in range(HOPS):
                    hop_in(c).wait_send()
                send_sketch(3)
                for c in range(CHUNKS):
                    r_copy(1, c).wait_send()
                for c in range(HOPS, CHUNKS):
                    r_copy(2, c).start()

            left_arrives(0)

            @pl.when(me == 1)
            def _():
                send_sketch(1)

            prepare_left(0)

        absorb_side(r, 1 - early)
        mid[...] = mm(l_turned[...], z[0])

        @pl.when((r == 0) & (me == 1))
        def _():
            send_sketch(2)

        @pl.when((r == 0) & (me == 3))
        def _():
            for k in range(1, NS):
                send_sketch(k)

        @pl.when(r < NS - 1)
        def _():
            relay(r + 1)

        for side in range(2):
            g_copy(r, side).wait_recv()
        for side in range(2):
            work[side, :, :W] = gram_in[r, side].astype(F32) + gram_own[1 - side] + eye
            work[side, :, W:] = eye
        prepare_right(jnp.minimum(r + 1, NS - 1))
        inverse_factors(work, inverse, mixed)

        @pl.when(r < NS - 1)
        def _():
            left_arrives(r + 1)
            prepare_left(r + 1)

        lefted = mm3(inverse[0], mid[...])
        for d in range(D):
            tall[pl.ds(d, W, stride=D), :] = lefted[:, d * W : (d + 1) * W]
        high, low = halves(inverse[1])
        second = jnp.concatenate([high, low, high], axis=1)
        high, low = halves(tall[...])
        fresh = mm_nt(jnp.concatenate([high, high, low], axis=1), second)
        scaling = lax.rsqrt(jnp.mean(fresh * fresh) + 1e-6)
        result = (fresh * scaling).astype(BF16)
        bm[r + 1] = result

        @pl.when(r != me)
        def _():
            o_copy(r).start()

        @pl.when(r == me)
        def _():
            o_stay(r).start()

        @pl.when(r < NS - 1)
        def _():
            sides[0] = result
            high, low = halves(lefted)
            for d in range(D):
                lanes_d = slice(d * W, (d + 1) * W)
                piece = jnp.concatenate([high[:, lanes_d], high[:, lanes_d], low[:, lanes_d]], axis=1)
                tall[pl.ds(d, W, stride=D), :] = mm_nt(second, piece)
            sides[1] = (tall[...] * scaling).astype(BF16)

        return carry

    lax.fori_loop(0, NS, absorb, 0)

    for c in range(CHUNKS):

        @pl.when(me != 0)
        def _():
            r_copy(1, c).wait_send()

        if c < HOPS:

            @pl.when(me != 0)
            def _():
                r_copy(2, c).wait_send()

            @pl.when(me == 3)
            def _():
                hop_on(c).wait_send()

        else:
            r_copy(2, c).wait_send()
        r_copy(3, c).wait_send()
        for r in range(NS):
            l_copy(r, c).wait_send()
    for k in range(1, NS):
        w_copy(k).wait_send()
    for r in range(NS):
        for side in range(2):
            g_copy(r, side).wait_send()

        @pl.when(r != me)
        def _():
            o_copy(r).wait_send()
            o_arrival(r).wait_recv()

    o_stay(me).wait()


def body(boundary, peps_rows, sketch, ranks, sizes, charges):
    any_space = pl.BlockSpec(memory_space=pl.ANY)
    smem = pl.BlockSpec(memory_space=pltpu.SMEM)
    vmem = pl.BlockSpec(memory_space=pltpu.VMEM)
    dma = pltpu.SemaphoreType.DMA
    result = pl.pallas_call(
        kernel,
        out_shape=jax.ShapeDtypeStruct((NS, W * D, W), BF16),
        in_specs=[vmem, smem, smem, smem, any_space, any_space],
        out_specs=any_space,
        scratch_shapes=[
            pltpu.VMEM((NS, W * D, W), BF16),
            pltpu.VMEM((NS + 1, W * D, W), BF16),
            pltpu.VMEM((2, W * D, W), BF16),
            pltpu.VMEM((NS, W * D, W), BF16),
            pltpu.VMEM((NS, W * D, W), BF16),
            pltpu.VMEM((2, W, W * D), BF16),
            pltpu.VMEM((W, W * D), BF16),
            pltpu.VMEM((64, W), F32),
            pltpu.VMEM((NS, 64, W), BF16),
            pltpu.VMEM((2, 256, 256), BF16),
            pltpu.VMEM((2, W * D, W * D), BF16),
            pltpu.VMEM((W, W * D), F32),
            pltpu.VMEM((W * D, W), F32),
            pltpu.VMEM((2, W, W), F32),
            pltpu.VMEM((NS, 2, W, W), BF16),
            pltpu.VMEM((NS, 2, W, W), BF16),
            pltpu.VMEM((2, W, 2 * W), F32),
            pltpu.VMEM((2, W, W), F32),
            pltpu.VMEM((W, 4 * W), F32),
            pltpu.VMEM((HOPS, CHUNK, W), BF16),
            dma((NS,)), dma(()), dma((NS - 1, CHUNKS)), dma((NS, CHUNKS)), dma((NS - 1,)),
            dma((NS,)), dma((NS, CHUNKS)), dma((NS, CHUNKS)), dma((NS, 2)), dma((NS, 2)),
            dma((NS,)), dma((NS,)), dma(()), dma((HOPS,)), dma((HOPS,)),
        ],
        compiler_params=pltpu.CompilerParams(
            collective_id=0, has_side_effects=True, vmem_limit_bytes=56 * 2**20
        ),
        name="absorb_rows",
    )(
        peps_rows.reshape(D * D, D, D),
        ranks.reshape(NS),
        sizes,
        charges,
        boundary.reshape(NS, W * D, W),
        sketch.reshape(NS, W * D, W),
    )
    return result.reshape(1, 1, NS, W, D, W)


def solution(mesh):
    placed = (
        P("col", None, None, None, None),
        P("row", "col", None, None, None, None),
        P("row", "col", None, None, None),
        P("row", "col", None),
        P(),
        P(),
    )
    return jax.shard_map(
        body,
        mesh=mesh,
        in_specs=placed,
        out_specs=P("row", "col", None, None, None, None),
        check_vma=False,
    )
```

```python
import jax
import jax.numpy as jnp
from jax import lax
from jax.experimental import pallas as pl
from jax.experimental.pallas import tpu as pltpu
from jax.sharding import PartitionSpec as P

W = 128
D = 8
NS = 4
CHUNKS = 4
HOPS = 2
CHUNK = W * D // CHUNKS
F32 = jnp.float32
BF16 = jnp.bfloat16
MESH = pl.DeviceIdType.MESH


def iota(shape, axis):
    return lax.broadcasted_iota(jnp.int32, shape, axis)


def mm(a, b):
    return jnp.dot(a, b, preferred_element_type=F32)


def mm_nt(a, b):
    return lax.dot_general(a, b, (((1,), (1,)), ((), ())), preferred_element_type=F32)


def mm_tn(a, b):
    return lax.dot_general(a, b, (((0,), (0,)), ((), ())), preferred_element_type=F32)


def compact_tensor(peps_ref, charges_ref, compact):
    rows = iota((512, 1), 0)
    l, h, u = rows >> 6, (rows >> 3) & 7, rows & 7
    balance = jnp.zeros((512, 1), jnp.int32)
    for i in range(D):
        q = charges_ref[i]
        balance += q * (
            (l == i).astype(jnp.int32) + (u == i).astype(jnp.int32) - (h == i).astype(jnp.int32)
        )
    values = peps_ref[...].astype(F32).reshape(512, D)
    big = iota((512, W), 0)
    lane = iota((512, W), 1)
    from_row = jnp.where(lane < 64, big & 63, ((big >> 6) << 3) | (big & 7))
    same = from_row == (lane & 63)
    pick = iota((2 * D, 512), 0)
    source = iota((2 * D, 512), 1)
    wanted = jnp.where(pick < D, source >> 6, (source >> 3) & 7)
    picker = (wanted == (pick & 7)).astype(BF16)
    for d in range(D):
        column = jnp.where(balance == charges_ref[d], values[:, d : d + 1], 0.0)
        spread = jnp.where(same, jnp.broadcast_to(column, (512, W)), 0.0).astype(BF16)
        both = mm(picker, spread)
        compact[pl.ds(d * D, D), :] = jnp.where(iota((D, W), 1) < 64, both[:D], both[D:])


def halves(x):
    high = x.astype(BF16)
    return high, (x - high.astype(F32)).astype(BF16)


def mm3(a, b):
    ah, al = halves(a)
    bh, bl = halves(b)
    return mm(jnp.concatenate([ah, ah, al], axis=1), jnp.concatenate([bh, bl, bh], axis=0))


def mm3_tn(a, b):
    ah, al = halves(a)
    bh, bl = halves(b)
    return mm_tn(jnp.concatenate([ah, ah, al], axis=0), jnp.concatenate([bh, bl, bh], axis=0))


def vreg(x):
    return jnp.broadcast_to(x, (8, W))


def eliminate(tiles, beyond, first, part):
    sub = iota((8, W), 0)
    groups = [list(tiles)] + ([list(beyond)] if beyond else [])

    def spread(v, j):
        a, b = (first[0] + j) % W, (first[1] + j) % W
        return jnp.where(part, vreg(v[:, a : a + 1]), vreg(v[:, b : b + 1]))

    def row(x, i):
        return vreg(x[i : i + 1, :])

    tiles = groups[0]
    own = [spread(tiles[0], t) for t in range(8)]
    for q in range(4):
        low = {o: [spread(tiles[o], 8 * q + t) for t in range(8)] for o in range(q + 1, 4)}
        after = [spread(tiles[q + 1], 8 * q + 8 + t) for t in range(8)] if q < 3 else []
        pivots = None
        for t in range(0, 8, 2):
            one, cross, two = row(own[t], t), row(own[t], t + 1), row(own[t + 1], t + 1)
            determinant = one * two - cross * cross
            over_one = 1.0 / one
            over_two = one * (1.0 / determinant)
            ratio = cross * over_one
            schur = determinant * over_one
            pivots = one if t == 0 else jnp.where(sub == t, one, pivots)
            pivots = jnp.where(sub == t + 1, schur, pivots)
            rows_one = {k: row(own[t], k) for k in range(t + 2, 8)}
            rows_two = {k: row(own[t + 1], k) - ratio * rows_one[k] for k in range(t + 2, 8)}
            factor_one = own[t] * over_one
            factor_two = (own[t + 1] - own[t] * ratio) * over_two
            for k in range(t + 2, 8):
                own[k] = (own[k] - factor_one * rows_one[k]) - factor_two * rows_two[k]
            factor_one = jnp.where(sub > t, factor_one, 0.0)
            factor_two = jnp.where(sub > t + 1, factor_two, 0.0)
            here = []
            for group in groups:
                upper = row(group[q], t)
                here.append((upper, row(group[q], t + 1) - ratio * upper))
            for o in range(q + 1, 4):
                second = low[o][t + 1] - low[o][t] * ratio
                below_one = low[o][t] * over_one
                below_two = second * over_two
                if o == q + 1:
                    for k in range(8):
                        after[k] = (after[k] - below_one * row(low[o][t], k)) - below_two * row(
                            second, k
                        )
                for k in range(t + 2, 8):
                    low[o][k] = (low[o][k] - below_one * rows_one[k]) - below_two * rows_two[k]
                for group, (upper, lower) in zip(groups, here):
                    group[o] = (group[o] - below_one * upper) - below_two * lower
            for group, (upper, lower) in zip(groups, here):
                group[q] = (group[q] - factor_one * upper) - factor_two * lower
        root = lax.rsqrt(pivots)
        for group in groups:
            group[q] = group[q] * root
        own = after
    return groups


def inverse_factors(work, inverse, mixed):
    lane, sub = iota((8, W), 1), iota((8, W), 0)
    group = lane >> 5
    ready = None
    for k in range(4):
        at = [(k + i) % 4 for i in range(4)]
        part = (group == at[0]) | (group == at[1])
        tiles, beyond = [], []
        for q in range(4):
            rows = pl.ds(32 * k + 8 * q, 8)
            one, two = work[0, rows, :W], pltpu.roll(work[1, rows, :W], 64, 1)
            if k < 3:
                beyond.append(jnp.where(group == at[1], one, jnp.where(group == at[3], two, 0.0)))
            if k > 0:
                one, two = ready[q]
            unit = ((lane & 31) == (sub + 8 * q)).astype(F32)
            tiles.append(jnp.where(group == at[0], one, jnp.where(group == at[2], two, unit)))
        done = eliminate(tiles, beyond, (32 * k, 32 * k + 64), part)
        if k < 3:
            ahead = jnp.concatenate(done[1], axis=0)
            update = mm3_tn(ahead, ahead)
            ready = []
            for q in range(4):
                rows = pl.ds(32 * (k + 1) + 8 * q, 8)
                one = work[0, rows, :W] - update[32 * at[1] + 8 * q : 32 * at[1] + 8 * q + 8]
                two = pltpu.roll(work[1, rows, :W], 64, 1)
                ready.append((one, two - update[32 * at[3] + 8 * q : 32 * at[3] + 8 * q + 8]))
        slot = k % 2
        mixed[slot] = jnp.zeros((W, 4 * W), F32)
        mixed[slot, pl.ds(32 * at[1], 32), : 2 * W] = work[0, pl.ds(32 * k, 32), :]
        mixed[slot, pl.ds(32 * at[3], 32), 2 * W :] = work[1, pl.ds(32 * k, 32), :]
        both = mm3(jnp.concatenate(done[0], axis=0), mixed[slot])
        for i in range(2):
            panel = both[:, i * 2 * W : (i + 1) * 2 * W]
            inverse[i, pl.ds(32 * k, 32), :] = panel[:, W:]
            if k < 3:
                below = 32 * (k + 1)
                update = mm3_tn(panel[:, :W], panel)
                work[i, pl.ds(below, W - below), :] -= update[below:, :]


def kernel(
    peps_ref, ranks_ref, sizes_ref, charges_ref, boundary_ref, sketch_ref, out_ref,
    sk, bm, sides, r_raw, l_raw, wides, l_turned, comp32, comp, kron, z, mid, tall,
    gram_own, gram_out, gram_in, work, inverse, mixed, hop, near, near_comp,
    sk_sem, b_sem, r_send, r_recv, w_send, w_recv, l_send, l_recv,
    g_send, g_recv, o_send, o_recv, o_local, hop_recv, hop_send,
    near_send, near_recv, near_on,
):
    me = lax.axis_index("row")
    col = lax.axis_index("col")
    cols = lax.axis_size("col")
    right = lax.rem(col + 1, cols)
    left = lax.rem(col + cols - 1, cols)

    def sketch_load(s):
        return pltpu.make_async_copy(sketch_ref.at[s], sk.at[s], sk_sem.at[s])

    def chunk(c):
        return pl.ds(c * CHUNK, CHUNK)

    def r_copy(k, c):
        s = lax.rem(me + k, NS)
        return pltpu.make_async_remote_copy(
            src_ref=sk.at[s, chunk(c)], dst_ref=r_raw.at[me, chunk(c)],
            send_sem=r_send.at[k - 1, c], recv_sem=r_recv.at[me, c],
            device_id=(s, col), device_id_type=MESH,
        )

    def r_arrival(r, c):
        return pltpu.make_async_remote_copy(
            src_ref=sk.at[0, chunk(c)], dst_ref=r_raw.at[r, chunk(c)],
            send_sem=r_send.at[0, c], recv_sem=r_recv.at[r, c],
            device_id=(me, col), device_id_type=MESH,
        )

    def l_copy(r, c):
        return pltpu.make_async_remote_copy(
            src_ref=r_raw.at[r, chunk(c)], dst_ref=l_raw.at[r, chunk(c)],
            send_sem=l_send.at[r, c], recv_sem=l_recv.at[r, c],
            device_id=(me, right), device_id_type=MESH,
        )

    def w_copy(k):
        s = lax.rem(me + k, NS)
        return pltpu.make_async_remote_copy(
            src_ref=comp.at[me], dst_ref=comp.at[me], send_sem=w_send.at[k - 1],
            recv_sem=w_recv.at[me], device_id=(s, col), device_id_type=MESH,
        )

    def w_arrival(r):
        return pltpu.make_async_remote_copy(
            src_ref=comp.at[r], dst_ref=comp.at[r], send_sem=w_send.at[0],
            recv_sem=w_recv.at[r], device_id=(me, col), device_id_type=MESH,
        )

    def g_copy(r, side):
        return pltpu.make_async_remote_copy(
            src_ref=gram_out.at[r, side], dst_ref=gram_in.at[r, side],
            send_sem=g_send.at[r, side], recv_sem=g_recv.at[r, side],
            device_id=(me, right + side * (left - right)), device_id_type=MESH,
        )

    def o_copy(r):
        return pltpu.make_async_remote_copy(
            src_ref=bm.at[r + 1], dst_ref=out_ref.at[me], send_sem=o_send.at[r],
            recv_sem=o_recv.at[me], device_id=(r, col), device_id_type=MESH,
        )

    def o_arrival(s):
        return pltpu.make_async_remote_copy(
            src_ref=bm.at[1], dst_ref=out_ref.at[s], send_sem=o_send.at[0],
            recv_sem=o_recv.at[s], device_id=(me, col), device_id_type=MESH,
        )

    def o_stay(r):
        return pltpu.make_async_copy(bm.at[r + 1], out_ref.at[me], o_local)

    def hop_in(c):
        return pltpu.make_async_remote_copy(
            src_ref=sk.at[2, chunk(c)], dst_ref=hop.at[c], send_sem=r_send.at[1, c],
            recv_sem=hop_recv.at[c], device_id=(3, col), device_id_type=MESH,
        )

    def hop_on(c):
        return pltpu.make_async_remote_copy(
            src_ref=hop.at[c], dst_ref=r_raw.at[0, chunk(c)], send_sem=hop_send.at[c],
            recv_sem=r_recv.at[0, c], device_id=(2, col), device_id_type=MESH,
        )

    def near_copy():
        return pltpu.make_async_remote_copy(
            src_ref=bm.at[0], dst_ref=near, send_sem=near_send.at[0], recv_sem=near_recv.at[0],
            device_id=(me, left), device_id_type=MESH,
        )

    def near_comp_copy():
        return pltpu.make_async_remote_copy(
            src_ref=comp.at[0], dst_ref=near_comp, send_sem=near_send.at[1],
            recv_sem=near_recv.at[1], device_id=(me, left), device_id_type=MESH,
        )

    def near_comp_on(k):
        return pltpu.make_async_remote_copy(
            src_ref=near_comp, dst_ref=near_comp, send_sem=near_on.at[k - 1],
            recv_sem=near_recv.at[1], device_id=(k, col), device_id_type=MESH,
        )

    def send_sketch(k):
        for c in range(CHUNKS):
            r_copy(k, c).start()

    barrier = pltpu.get_barrier_semaphore()
    for k in range(1, NS):
        pl.semaphore_signal(
            barrier, inc=1, device_id=(lax.rem(me + k, NS), col), device_id_type=MESH
        )
    for c in (left, right):
        pl.semaphore_signal(barrier, inc=1, device_id=(me, c), device_id_type=MESH)
    for s in range(NS):
        sketch_load(s).start()
    boundary_load = pltpu.make_async_copy(boundary_ref.at[me], bm.at[0], b_sem)
    boundary_load.start()
    lanes = iota((1, W), 1)
    for s in range(NS):
        sketch_load(s).wait()
        sk[s] = sk[s] * (lanes < ranks_ref[s]).astype(BF16)
    r_raw[me] = sk[me]
    pl.semaphore_wait(barrier, NS + 1)

    @pl.when(me == 0)
    def _():
        send_sketch(1)
        for c in range(HOPS):
            hop_in(c).start()

    @pl.when(me == 1)
    def _():
        send_sketch(3)

    @pl.when(me == 2)
    def _():
        send_sketch(1)
        send_sketch(3)
        send_sketch(2)

    boundary_load.wait()
    near_copy().start()
    compact_tensor(peps_ref, charges_ref, comp32)
    comp[me] = comp32[...].astype(BF16)

    @pl.when(me == 0)
    def _():
        near_comp_copy().start()

    for k in range(1, NS):
        w_copy(k).start()

    block = iota((256, 256), 0) >> 6 == iota((256, 256), 1) >> 6

    def relay(r):
        for c in range(CHUNKS):

            @pl.when(r != me)
            def _():
                r_arrival(r, c).wait_recv()

            l_copy(r, c).start()

        @pl.when(r != me)
        def _():
            w_arrival(r).wait_recv()

    def regroup(side, natural):
        tall[...] = natural
        for h in range(D):
            wides[side, :, h * W : (h + 1) * W] = tall[pl.ds(h, W, stride=D), :].astype(BF16)

    def expand(both, slots):
        turned = pltpu.roll(both, 64, 1)
        low = iota((64, W), 1) < 64
        for i, slot in slots:
            twice = jnp.where(low, both, turned) if i == 0 else jnp.where(low, turned, both)
            four = jnp.concatenate([twice, twice], axis=1)
            kron[slot] = jnp.where(block, jnp.concatenate([four] * 4, axis=0), 0.0).astype(BF16)

    def prepare_right(r):
        regroup(0, r_raw[r].astype(F32))
        expand(comp[r].astype(F32), ((0, 0), (1, 1)))

    def prepare_left(r):
        natural = l_raw[r].astype(F32)
        regroup(1, natural)
        l_turned[...] = natural.T.astype(BF16)

    def left_arrives(r):
        for c in range(CHUNKS):
            l_copy(r, c).wait_recv()

    def absorb_side(lhs, wide, side):
        part = mm(sides[lhs], wides[wide])
        columns = []
        for q in range(W // 4):
            pieces = [
                part[(4 * q + i) * D : (4 * q + i + 1) * D, h * W : (h + 1) * W]
                for i in range(4)
                for h in range(D)
            ]
            columns.append(jnp.concatenate(pieces, axis=0).astype(BF16))
        whole = mm(kron[lhs], jnp.concatenate(columns, axis=1))
        for d in range(D):
            pieces = [
                whole[(i * D + d) * D : (i * D + d + 1) * D, q * W : (q + 1) * W]
                for q in range(W // 4)
                for i in range(4)
            ]
            z[side, :, d * W : (d + 1) * W] = jnp.concatenate(pieces, axis=0).astype(BF16)
        gram = jnp.zeros((W, W), F32)
        for d in range(D):
            piece = z[side, :, d * W : (d + 1) * W]
            gram += mm_tn(piece, piece)
        gram_own[side] = gram

    def send_gram(r, side):
        gram_out[r, side] = gram_own[side].astype(BF16)
        g_copy(r, side).start()

    def masked(block):
        size = sizes_ref[me]
        inside = ((iota((W * D, W), 0) >> 3) < size) & (iota((W * D, W), 1) < size)
        return jnp.where(inside, block.astype(F32), 0.0)

    def turn_side(start, side):
        tall[...] = start
        for u in range(D):
            mid[:, u * W : (u + 1) * W] = tall[pl.ds(u, W, stride=D), :].T
        for u in range(D):
            tall[pl.ds(u, W, stride=D), :] = mid[:, u * W : (u + 1) * W]
        sides[side] = tall[...].astype(BF16)

    def prepare_near():
        near_copy().wait_recv()
        turn_side(masked(near[...]), 2)

    sides[0] = masked(bm[0]).astype(BF16)

    @pl.when(me != 0)
    def _():
        prepare_near()

    @pl.when(me == 3)
    def _():
        for c in range(HOPS):
            hop_in(c).wait_recv()
            hop_on(c).start()

    relay(0)
    prepare_right(0)

    eye = (iota((W, W), 0) == iota((W, W), 1)).astype(F32)

    def absorb(r, carry):
        first_row = r == 0
        early = jnp.where(first_row, 0, 1 - lax.rem(col, 2))
        absorb_side(early, early, early)

        @pl.when(first_row)
        def _():
            @pl.when(me == 0)
            def _():
                for c in range(HOPS):
                    hop_in(c).wait_send()
                send_sketch(3)
                for c in range(CHUNKS):
                    r_copy(1, c).wait_send()
                for c in range(HOPS, CHUNKS):
                    r_copy(2, c).start()
                near_comp_copy().wait_recv()
                for k in range(1, NS):
                    near_comp_on(k).start()
                prepare_near()

            @pl.when(me != 0)
            def _():
                near_comp_copy().wait_recv()

            expand(near_comp[...].astype(F32), ((1, 2),))

        @pl.when(jnp.logical_not(first_row))
        def _():
            send_gram(r, early)

        absorb_side(
            jnp.where(first_row, 2, 1 - early), jnp.where(first_row, 0, 1 - early), 1 - early
        )

        @pl.when(first_row)
        def _():
            gram_out[0, 0] = (gram_own[0] + gram_own[1]).astype(BF16)
            g_copy(0, 0).start()
            gram_in[0, 1] = gram_own[1].astype(BF16)
            gram_own[1] = jnp.zeros((W, W), F32)

            @pl.when(me == 1)
            def _():
                send_sketch(1)

            left_arrives(0)
            l_turned[...] = l_raw[0].astype(F32).T.astype(BF16)

        @pl.when(jnp.logical_not(first_row))
        def _():
            send_gram(r, 1 - early)

        mid[...] = mm(l_turned[...], z[0])

        @pl.when((r == 0) & (me == 1))
        def _():
            send_sketch(2)

        @pl.when((r == 0) & (me == 3))
        def _():
            for k in range(1, NS):
                send_sketch(k)

        @pl.when(r == 0)
        def _():
            relay(1)

        @pl.when((r > 0) & (r < NS - 1))
        def _():
            left_arrives(r + 1)
            prepare_left(r + 1)

        g_copy(r, 0).wait_recv()

        @pl.when(r > 0)
        def _():
            g_copy(r, 1).wait_recv()

        for side in range(2):
            work[side, :, :W] = gram_in[r, side].astype(F32) + gram_own[1 - side] + eye
            work[side, :, W:] = eye
        prepare_right(jnp.minimum(r + 1, NS - 1))
        inverse_factors(work, inverse, mixed)

        @pl.when(r < NS - 2)
        def _():
            relay(r + 2)

        @pl.when(r == 0)
        def _():
            left_arrives(1)
            prepare_left(1)

        lefted = mm3(inverse[0], mid[...])
        for d in range(D):
            tall[pl.ds(d, W, stride=D), :] = lefted[:, d * W : (d + 1) * W]
        high, low = halves(inverse[1])
        second = jnp.concatenate([high, low, high], axis=1)
        high, low = halves(tall[...])
        fresh = mm_nt(jnp.concatenate([high, high, low], axis=1), second)
        scaling = lax.rsqrt(jnp.mean(fresh * fresh) + 1e-6)
        result = (fresh * scaling).astype(BF16)
        bm[r + 1] = result

        @pl.when(r != me)
        def _():
            o_copy(r).start()

        @pl.when(r == me)
        def _():
            o_stay(r).start()

        @pl.when(r < NS - 1)
        def _():
            sides[0] = result
            high, low = halves(lefted)
            for d in range(D):
                lanes_d = slice(d * W, (d + 1) * W)
                piece = jnp.concatenate([high[:, lanes_d], high[:, lanes_d], low[:, lanes_d]], axis=1)
                tall[pl.ds(d, W, stride=D), :] = mm_nt(second, piece)
            sides[1] = (tall[...] * scaling).astype(BF16)

        return carry

    lax.fori_loop(0, NS, absorb, 0)

    for c in range(CHUNKS):

        @pl.when(me != 0)
        def _():
            r_copy(1, c).wait_send()

        if c < HOPS:

            @pl.when(me != 0)
            def _():
                r_copy(2, c).wait_send()

            @pl.when(me == 3)
            def _():
                hop_on(c).wait_send()

        else:
            r_copy(2, c).wait_send()
        r_copy(3, c).wait_send()
        for r in range(NS):
            l_copy(r, c).wait_send()
    for k in range(1, NS):
        w_copy(k).wait_send()
    near_copy().wait_send()

    @pl.when(me == 0)
    def _():
        near_comp_copy().wait_send()
        for k in range(1, NS):
            near_comp_on(k).wait_send()

    for r in range(NS):
        g_copy(r, 0).wait_send()
        if r > 0:
            g_copy(r, 1).wait_send()

        @pl.when(r != me)
        def _():
            o_copy(r).wait_send()
            o_arrival(r).wait_recv()

    o_stay(me).wait()


def body(boundary, peps_rows, sketch, ranks, sizes, charges):
    any_space = pl.BlockSpec(memory_space=pl.ANY)
    smem = pl.BlockSpec(memory_space=pltpu.SMEM)
    vmem = pl.BlockSpec(memory_space=pltpu.VMEM)
    dma = pltpu.SemaphoreType.DMA
    result = pl.pallas_call(
        kernel,
        out_shape=jax.ShapeDtypeStruct((NS, W * D, W), BF16),
        in_specs=[vmem, smem, smem, smem, any_space, any_space],
        out_specs=any_space,
        scratch_shapes=[
            pltpu.VMEM((NS, W * D, W), BF16),
            pltpu.VMEM((NS + 1, W * D, W), BF16),
            pltpu.VMEM((3, W * D, W), BF16),
            pltpu.VMEM((NS, W * D, W), BF16),
            pltpu.VMEM((NS, W * D, W), BF16),
            pltpu.VMEM((2, W, W * D), BF16),
            pltpu.VMEM((W, W * D), BF16),
            pltpu.VMEM((64, W), F32),
            pltpu.VMEM((NS, 64, W), BF16),
            pltpu.VMEM((3, 256, 256), BF16),
            pltpu.VMEM((2, W * D, W * D), BF16),
            pltpu.VMEM((W, W * D), F32),
            pltpu.VMEM((W * D, W), F32),
            pltpu.VMEM((2, W, W), F32),
            pltpu.VMEM((NS, 2, W, W), BF16),
            pltpu.VMEM((NS, 2, W, W), BF16),
            pltpu.VMEM((2, W, 2 * W), F32),
            pltpu.VMEM((2, W, W), F32),
            pltpu.VMEM((2, W, 4 * W), F32),
            pltpu.VMEM((HOPS, CHUNK, W), BF16),
            pltpu.VMEM((W * D, W), BF16),
            pltpu.VMEM((64, W), BF16),
            dma((NS,)), dma(()), dma((NS - 1, CHUNKS)), dma((NS, CHUNKS)), dma((NS - 1,)),
            dma((NS,)), dma((NS, CHUNKS)), dma((NS, CHUNKS)), dma((NS, 2)), dma((NS, 2)),
            dma((NS,)), dma((NS,)), dma(()), dma((HOPS,)), dma((HOPS,)),
            dma((2,)), dma((2,)), dma((NS - 1,)),
        ],
        compiler_params=pltpu.CompilerParams(
            collective_id=0, has_side_effects=True, vmem_limit_bytes=56 * 2**20
        ),
        name="absorb_rows",
    )(
        peps_rows.reshape(D * D, D, D),
        ranks.reshape(NS),
        sizes,
        charges,
        boundary.reshape(NS, W * D, W),
        sketch.reshape(NS, W * D, W),
    )
    return result.reshape(1, 1, NS, W, D, W)


def solution(mesh):
    placed = (
        P("col", None, None, None, None),
        P("row", "col", None, None, None, None),
        P("row", "col", None, None, None),
        P("row", "col", None),
        P(),
        P(),
    )
    return jax.shard_map(
        body,
        mesh=mesh,
        in_specs=placed,
        out_specs=P("row", "col", None, None, None, None),
        check_vma=False,
    )
```

```python
import jax
import jax.numpy as jnp
from jax import lax
from jax.experimental import pallas as pl
from jax.experimental.pallas import tpu as pltpu
from jax.sharding import PartitionSpec as P

W = 128
D = 8
NS = 4
CHUNKS = 4
HOPS = 2
CHUNK = W * D // CHUNKS
F32 = jnp.float32
BF16 = jnp.bfloat16
MESH = pl.DeviceIdType.MESH


def iota(shape, axis):
    return lax.broadcasted_iota(jnp.int32, shape, axis)


def mm(a, b):
    return jnp.dot(a, b, preferred_element_type=F32)


def mm_nt(a, b):
    return lax.dot_general(a, b, (((1,), (1,)), ((), ())), preferred_element_type=F32)


def mm_tn(a, b):
    return lax.dot_general(a, b, (((0,), (0,)), ((), ())), preferred_element_type=F32)


def compact_tensor(peps_ref, charges_ref, compact):
    rows = iota((512, 1), 0)
    l, h, u = rows >> 6, (rows >> 3) & 7, rows & 7
    balance = jnp.zeros((512, 1), jnp.int32)
    for i in range(D):
        q = charges_ref[i]
        balance += q * (
            (l == i).astype(jnp.int32) + (u == i).astype(jnp.int32) - (h == i).astype(jnp.int32)
        )
    values = peps_ref[...].astype(F32).reshape(512, D)
    big = iota((512, W), 0)
    lane = iota((512, W), 1)
    from_row = jnp.where(lane < 64, big & 63, ((big >> 6) << 3) | (big & 7))
    same = from_row == (lane & 63)
    pick = iota((2 * D, 512), 0)
    source = iota((2 * D, 512), 1)
    wanted = jnp.where(pick < D, source >> 6, (source >> 3) & 7)
    picker = (wanted == (pick & 7)).astype(BF16)
    for d in range(D):
        column = jnp.where(balance == charges_ref[d], values[:, d : d + 1], 0.0)
        spread = jnp.where(same, jnp.broadcast_to(column, (512, W)), 0.0).astype(BF16)
        both = mm(picker, spread)
        compact[pl.ds(d * D, D), :] = jnp.where(iota((D, W), 1) < 64, both[:D], both[D:])


def halves(x):
    high = x.astype(BF16)
    return high, (x - high.astype(F32)).astype(BF16)


def mm3(a, b):
    ah, al = halves(a)
    bh, bl = halves(b)
    return mm(jnp.concatenate([ah, ah, al], axis=1), jnp.concatenate([bh, bl, bh], axis=0))


def mm3_tn(a, b):
    ah, al = halves(a)
    bh, bl = halves(b)
    return mm_tn(jnp.concatenate([ah, ah, al], axis=0), jnp.concatenate([bh, bl, bh], axis=0))


def vreg(x):
    return jnp.broadcast_to(x, (8, W))


def eliminate(tiles, beyond, first, part):
    sub = iota((8, W), 0)
    groups = [list(tiles)] + ([list(beyond)] if beyond else [])

    def spread(v, j):
        a, b = (first[0] + j) % W, (first[1] + j) % W
        return jnp.where(part, vreg(v[:, a : a + 1]), vreg(v[:, b : b + 1]))

    def row(x, i):
        return vreg(x[i : i + 1, :])

    tiles = groups[0]
    own = [spread(tiles[0], t) for t in range(8)]
    for q in range(4):
        low = {o: [spread(tiles[o], 8 * q + t) for t in range(8)] for o in range(q + 1, 4)}
        after = [spread(tiles[q + 1], 8 * q + 8 + t) for t in range(8)] if q < 3 else []
        pivots = None
        for t in range(0, 8, 2):
            one, cross, two = row(own[t], t), row(own[t], t + 1), row(own[t + 1], t + 1)
            determinant = one * two - cross * cross
            over_one = 1.0 / one
            over_two = one * (1.0 / determinant)
            ratio = cross * over_one
            schur = determinant * over_one
            pivots = one if t == 0 else jnp.where(sub == t, one, pivots)
            pivots = jnp.where(sub == t + 1, schur, pivots)
            rows_one = {k: row(own[t], k) for k in range(t + 2, 8)}
            rows_two = {k: row(own[t + 1], k) - ratio * rows_one[k] for k in range(t + 2, 8)}
            factor_one = own[t] * over_one
            factor_two = (own[t + 1] - own[t] * ratio) * over_two
            for k in range(t + 2, 8):
                own[k] = (own[k] - factor_one * rows_one[k]) - factor_two * rows_two[k]
            factor_one = jnp.where(sub > t, factor_one, 0.0)
            factor_two = jnp.where(sub > t + 1, factor_two, 0.0)
            here = []
            for group in groups:
                upper = row(group[q], t)
                here.append((upper, row(group[q], t + 1) - ratio * upper))
            for o in range(q + 1, 4):
                second = low[o][t + 1] - low[o][t] * ratio
                below_one = low[o][t] * over_one
                below_two = second * over_two
                if o == q + 1:
                    for k in range(8):
                        after[k] = (after[k] - below_one * row(low[o][t], k)) - below_two * row(
                            second, k
                        )
                for k in range(t + 2, 8):
                    low[o][k] = (low[o][k] - below_one * rows_one[k]) - below_two * rows_two[k]
                for group, (upper, lower) in zip(groups, here):
                    group[o] = (group[o] - below_one * upper) - below_two * lower
            for group, (upper, lower) in zip(groups, here):
                group[q] = (group[q] - factor_one * upper) - factor_two * lower
        root = lax.rsqrt(pivots)
        for group in groups:
            group[q] = group[q] * root
        own = after
    return groups


def inverse_factors(work, inverse, mixed):
    lane, sub = iota((8, W), 1), iota((8, W), 0)
    group = lane >> 5
    ready = None
    for k in range(4):
        at = [(k + i) % 4 for i in range(4)]
        part = (group == at[0]) | (group == at[1])
        tiles, beyond = [], []
        for q in range(4):
            rows = pl.ds(32 * k + 8 * q, 8)
            one, two = work[0, rows, :W], pltpu.roll(work[1, rows, :W], 64, 1)
            if k < 3:
                beyond.append(jnp.where(group == at[1], one, jnp.where(group == at[3], two, 0.0)))
            if k > 0:
                one, two = ready[q]
            unit = ((lane & 31) == (sub + 8 * q)).astype(F32)
            tiles.append(jnp.where(group == at[0], one, jnp.where(group == at[2], two, unit)))
        done = eliminate(tiles, beyond, (32 * k, 32 * k + 64), part)
        if k < 3:
            ahead = jnp.concatenate(done[1], axis=0)
            update = mm3_tn(ahead, ahead)
            ready = []
            for q in range(4):
                rows = pl.ds(32 * (k + 1) + 8 * q, 8)
                one = work[0, rows, :W] - update[32 * at[1] + 8 * q : 32 * at[1] + 8 * q + 8]
                two = pltpu.roll(work[1, rows, :W], 64, 1)
                ready.append((one, two - update[32 * at[3] + 8 * q : 32 * at[3] + 8 * q + 8]))
        slot = k % 2
        mixed[slot] = jnp.zeros((W, 4 * W), F32)
        mixed[slot, pl.ds(32 * at[1], 32), : 2 * W] = work[0, pl.ds(32 * k, 32), :]
        mixed[slot, pl.ds(32 * at[3], 32), 2 * W :] = work[1, pl.ds(32 * k, 32), :]
        both = mm3(jnp.concatenate(done[0], axis=0), mixed[slot])
        for i in range(2):
            panel = both[:, i * 2 * W : (i + 1) * 2 * W]
            inverse[i, pl.ds(32 * k, 32), :] = panel[:, W:]
            if k < 3:
                below = 32 * (k + 1)
                update = mm3_tn(panel[:, :W], panel)
                work[i, pl.ds(below, W - below), :] -= update[below:, :]


def kernel(
    peps_ref, ranks_ref, sizes_ref, charges_ref, boundary_ref, sketch_ref, out_ref,
    sk, bm, sides, r_raw, l_raw, wides, l_turned, comp32, comp, kron, z, mid, tall,
    gram_own, gram_out, gram_in, work, inverse, mixed, hop, near, near_comp, turned,
    sk_sem, b_sem, r_send, r_recv, w_send, w_recv, l_send, l_recv,
    g_send, g_recv, o_send, o_recv, o_local, hop_recv, hop_send,
    near_send, near_recv, near_on,
):
    me = lax.axis_index("row")
    col = lax.axis_index("col")
    cols = lax.axis_size("col")
    right = lax.rem(col + 1, cols)
    left = lax.rem(col + cols - 1, cols)

    def sketch_load(s):
        return pltpu.make_async_copy(sketch_ref.at[s], sk.at[s], sk_sem.at[s])

    def chunk(c):
        return pl.ds(c * CHUNK, CHUNK)

    def r_copy(k, c):
        s = lax.rem(me + k, NS)
        return pltpu.make_async_remote_copy(
            src_ref=sk.at[s, chunk(c)], dst_ref=r_raw.at[me, chunk(c)],
            send_sem=r_send.at[k - 1, c], recv_sem=r_recv.at[me, c],
            device_id=(s, col), device_id_type=MESH,
        )

    def r_arrival(r, c):
        return pltpu.make_async_remote_copy(
            src_ref=sk.at[0, chunk(c)], dst_ref=r_raw.at[r, chunk(c)],
            send_sem=r_send.at[0, c], recv_sem=r_recv.at[r, c],
            device_id=(me, col), device_id_type=MESH,
        )

    def l_copy(r, c):
        return pltpu.make_async_remote_copy(
            src_ref=r_raw.at[r, chunk(c)], dst_ref=l_raw.at[r, chunk(c)],
            send_sem=l_send.at[r, c], recv_sem=l_recv.at[r, c],
            device_id=(me, right), device_id_type=MESH,
        )

    def w_copy(k):
        s = lax.rem(me + k, NS)
        return pltpu.make_async_remote_copy(
            src_ref=comp.at[me], dst_ref=comp.at[me], send_sem=w_send.at[k - 1],
            recv_sem=w_recv.at[me], device_id=(s, col), device_id_type=MESH,
        )

    def w_arrival(r):
        return pltpu.make_async_remote_copy(
            src_ref=comp.at[r], dst_ref=comp.at[r], send_sem=w_send.at[0],
            recv_sem=w_recv.at[r], device_id=(me, col), device_id_type=MESH,
        )

    def g_copy(r, side):
        return pltpu.make_async_remote_copy(
            src_ref=gram_out.at[r, side], dst_ref=gram_in.at[r, side],
            send_sem=g_send.at[r, side], recv_sem=g_recv.at[r, side],
            device_id=(me, right + side * (left - right)), device_id_type=MESH,
        )

    def o_copy(r):
        return pltpu.make_async_remote_copy(
            src_ref=bm.at[r + 1], dst_ref=out_ref.at[me], send_sem=o_send.at[r],
            recv_sem=o_recv.at[me], device_id=(r, col), device_id_type=MESH,
        )

    def o_arrival(s):
        return pltpu.make_async_remote_copy(
            src_ref=bm.at[1], dst_ref=out_ref.at[s], send_sem=o_send.at[0],
            recv_sem=o_recv.at[s], device_id=(me, col), device_id_type=MESH,
        )

    def o_stay(r):
        return pltpu.make_async_copy(bm.at[r + 1], out_ref.at[me], o_local)

    def hop_in(c):
        return pltpu.make_async_remote_copy(
            src_ref=sk.at[2, chunk(c)], dst_ref=hop.at[c], send_sem=r_send.at[1, c],
            recv_sem=hop_recv.at[c], device_id=(3, col), device_id_type=MESH,
        )

    def hop_on(c):
        return pltpu.make_async_remote_copy(
            src_ref=hop.at[c], dst_ref=r_raw.at[0, chunk(c)], send_sem=hop_send.at[c],
            recv_sem=r_recv.at[0, c], device_id=(2, col), device_id_type=MESH,
        )

    def near_copy():
        return pltpu.make_async_remote_copy(
            src_ref=bm.at[0], dst_ref=near, send_sem=near_send.at[0], recv_sem=near_recv.at[0],
            device_id=(me, left), device_id_type=MESH,
        )

    def near_comp_copy():
        return pltpu.make_async_remote_copy(
            src_ref=comp.at[0], dst_ref=near_comp, send_sem=near_send.at[1],
            recv_sem=near_recv.at[1], device_id=(me, left), device_id_type=MESH,
        )

    def near_comp_on(k):
        return pltpu.make_async_remote_copy(
            src_ref=near_comp, dst_ref=near_comp, send_sem=near_on.at[k - 1],
            recv_sem=near_recv.at[1], device_id=(k, col), device_id_type=MESH,
        )

    def send_result(r):
        @pl.when(r != me)
        def _():
            o_copy(r).start()

        @pl.when(r == me)
        def _():
            o_stay(r).start()

    def send_sketch(k):
        for c in range(CHUNKS):
            r_copy(k, c).start()

    barrier = pltpu.get_barrier_semaphore()
    for k in range(1, NS):
        pl.semaphore_signal(
            barrier, inc=1, device_id=(lax.rem(me + k, NS), col), device_id_type=MESH
        )
    for c in (left, right):
        pl.semaphore_signal(barrier, inc=1, device_id=(me, c), device_id_type=MESH)
    away = [lax.rem(me + k, NS) for k in (1, 2, 3, 0)]
    for s in away:
        sketch_load(s).start()
    boundary_load = pltpu.make_async_copy(boundary_ref.at[me], bm.at[0], b_sem)
    boundary_load.start()
    lanes = iota((1, W), 1)

    def mask_sketch(s):
        sketch_load(s).wait()
        sk[s] = sk[s] * (lanes < ranks_ref[s]).astype(BF16)

    mask_sketch(away[0])
    mask_sketch(away[1])
    pl.semaphore_wait(barrier, NS + 1)

    @pl.when(me == 0)
    def _():
        send_sketch(1)
        for c in range(HOPS):
            hop_in(c).start()

    mask_sketch(away[2])
    mask_sketch(away[3])
    r_raw[me] = sk[me]

    @pl.when(me == 1)
    def _():
        send_sketch(3)

    @pl.when(me == 2)
    def _():
        send_sketch(1)
        send_sketch(3)
        send_sketch(2)

    boundary_load.wait()
    near_copy().start()
    compact_tensor(peps_ref, charges_ref, comp32)
    comp[me] = comp32[...].astype(BF16)

    @pl.when(me == 0)
    def _():
        near_comp_copy().start()

    for k in range(1, NS):
        w_copy(k).start()

    block = iota((256, 256), 0) >> 6 == iota((256, 256), 1) >> 6

    def relay(r):
        for c in range(CHUNKS):

            @pl.when(r != me)
            def _():
                r_arrival(r, c).wait_recv()

            l_copy(r, c).start()

        @pl.when(r != me)
        def _():
            w_arrival(r).wait_recv()

    def regroup(side, natural):
        tall[...] = natural
        for h in range(D):
            wides[side, :, h * W : (h + 1) * W] = tall[pl.ds(h, W, stride=D), :].astype(BF16)

    def expand(both, slots):
        rolled = pltpu.roll(both, 64, 1)
        low = iota((64, W), 1) < 64
        for i, slot in slots:
            twice = jnp.where(low, both, rolled) if i == 0 else jnp.where(low, rolled, both)
            four = jnp.concatenate([twice, twice], axis=1)
            kron[slot] = jnp.where(block, jnp.concatenate([four] * 4, axis=0), 0.0).astype(BF16)

    def prepare_right(r):
        regroup(0, r_raw[r].astype(F32))
        expand(comp[r].astype(F32), ((0, 0), (1, 1)))

    def prepare_left(r):
        natural = l_raw[r].astype(F32)
        regroup(1, natural)
        l_turned[...] = natural.T.astype(BF16)

    def left_arrives(r):
        for c in range(CHUNKS):
            l_copy(r, c).wait_recv()

    def absorb_side(lhs, wide, side):
        part = mm(sides[lhs], wides[wide])
        columns = []
        for q in range(W // 4):
            pieces = [
                part[(4 * q + i) * D : (4 * q + i + 1) * D, h * W : (h + 1) * W]
                for i in range(4)
                for h in range(D)
            ]
            columns.append(jnp.concatenate(pieces, axis=0).astype(BF16))
        whole = mm(kron[lhs], jnp.concatenate(columns, axis=1))
        for d in range(D):
            pieces = [
                whole[(i * D + d) * D : (i * D + d + 1) * D, q * W : (q + 1) * W]
                for q in range(W // 4)
                for i in range(4)
            ]
            z[side, :, d * W : (d + 1) * W] = jnp.concatenate(pieces, axis=0).astype(BF16)
        gram = jnp.zeros((W, W), F32)
        for d in range(D):
            piece = z[side, :, d * W : (d + 1) * W]
            gram += mm_tn(piece, piece)
        gram_own[side] = gram

    def send_gram(r, side):
        gram_out[r, side] = gram_own[side].astype(BF16)
        g_copy(r, side).start()

    def masked(block):
        size = sizes_ref[me]
        inside = ((iota((W * D, W), 0) >> 3) < size) & (iota((W * D, W), 1) < size)
        return jnp.where(inside, block.astype(F32), 0.0)

    def turn_side(start, side):
        tall[...] = start
        for u in range(D):
            mid[:, u * W : (u + 1) * W] = tall[pl.ds(u, W, stride=D), :].T
        for u in range(D):
            tall[pl.ds(u, W, stride=D), :] = mid[:, u * W : (u + 1) * W]
        sides[side] = tall[...].astype(BF16)

    def prepare_near():
        near_copy().wait_recv()
        turn_side(masked(near[...]), 2)

    sides[0] = masked(bm[0]).astype(BF16)

    @pl.when(me != 0)
    def _():
        prepare_near()

    @pl.when(me == 3)
    def _():
        for c in range(HOPS):
            hop_in(c).wait_recv()
            hop_on(c).start()

    relay(0)
    prepare_right(0)

    eye = (iota((W, W), 0) == iota((W, W), 1)).astype(F32)

    def absorb(r, carry):
        first_row = r == 0
        early = jnp.where(first_row, 0, 1 - lax.rem(col, 2))
        absorb_side(early, early, early)

        @pl.when(first_row)
        def _():
            @pl.when(me == 0)
            def _():
                for c in range(HOPS):
                    hop_in(c).wait_send()
                send_sketch(3)
                for c in range(CHUNKS):
                    r_copy(1, c).wait_send()
                for c in range(HOPS, CHUNKS):
                    r_copy(2, c).start()
                near_comp_copy().wait_recv()
                for k in range(1, NS):
                    near_comp_on(k).start()
                prepare_near()

            @pl.when(me != 0)
            def _():
                near_comp_copy().wait_recv()

            expand(near_comp[...].astype(F32), ((1, 2),))

        @pl.when(jnp.logical_not(first_row))
        def _():
            send_gram(r, early)

        absorb_side(
            jnp.where(first_row, 2, 1 - early), jnp.where(first_row, 0, 1 - early), 1 - early
        )

        @pl.when(first_row)
        def _():
            gram_out[0, 0] = (gram_own[0] + gram_own[1]).astype(BF16)
            g_copy(0, 0).start()
            gram_in[0, 1] = gram_own[1].astype(BF16)
            gram_own[1] = jnp.zeros((W, W), F32)

            @pl.when(me == 1)
            def _():
                send_sketch(1)

            left_arrives(0)
            l_turned[...] = l_raw[0].astype(F32).T.astype(BF16)

        @pl.when(jnp.logical_not(first_row))
        def _():
            send_gram(r, 1 - early)

        mid[...] = mm(l_turned[...], z[0])

        @pl.when((r == 0) & (me == 1))
        def _():
            send_sketch(2)

        @pl.when((r == 0) & (me == 3))
        def _():
            for k in range(1, NS):
                send_sketch(k)

        @pl.when(r == 0)
        def _():
            relay(1)

        @pl.when((r > 0) & (r < NS - 1))
        def _():
            left_arrives(r + 1)
            prepare_left(r + 1)

        g_copy(r, 0).wait_recv()

        @pl.when(r > 0)
        def _():
            g_copy(r, 1).wait_recv()

        for side in range(2):
            work[side, :, :W] = gram_in[r, side].astype(F32) + gram_own[1 - side] + eye
            work[side, :, W:] = eye
        prepare_right(jnp.minimum(r + 1, NS - 1))
        inverse_factors(work, inverse, mixed)

        @pl.when(r < NS - 2)
        def _():
            relay(r + 2)

        @pl.when(r == 0)
        def _():
            left_arrives(1)
            prepare_left(1)

        def solved():
            lefted = mm3(inverse[0], mid[...])
            for d in range(D):
                tall[pl.ds(d, W, stride=D), :] = lefted[:, d * W : (d + 1) * W]
            high, low = halves(inverse[1])
            second = jnp.concatenate([high, low, high], axis=1)
            high, low = halves(tall[...])
            fresh = mm_nt(jnp.concatenate([high, high, low], axis=1), second)
            return lefted, second, fresh, lax.rsqrt(jnp.mean(fresh * fresh) + 1e-6)

        @pl.when(r < NS - 1)
        def _():
            lefted, second, fresh, scaling = solved()
            high, low = halves(lefted)
            for d in range(D):
                lanes_d = slice(d * W, (d + 1) * W)
                piece = jnp.concatenate([high[:, lanes_d], high[:, lanes_d], low[:, lanes_d]], axis=1)
                turned[pl.ds(d, W, stride=D), :] = mm_nt(second, piece)
            result = (fresh * scaling).astype(BF16)
            sides[0] = result
            bm[r + 1] = result
            sides[1] = (turned[...] * scaling).astype(BF16)
            send_result(r)

        @pl.when(r == NS - 1)
        def _():
            _, _, fresh, scaling = solved()
            bm[r + 1] = (fresh * scaling).astype(BF16)
            send_result(r)

        return carry

    lax.fori_loop(0, NS, absorb, 0)

    for c in range(CHUNKS):

        @pl.when(me != 0)
        def _():
            r_copy(1, c).wait_send()

        if c < HOPS:

            @pl.when(me != 0)
            def _():
                r_copy(2, c).wait_send()

            @pl.when(me == 3)
            def _():
                hop_on(c).wait_send()

        else:
            r_copy(2, c).wait_send()
        r_copy(3, c).wait_send()
        for r in range(NS):
            l_copy(r, c).wait_send()
    for k in range(1, NS):
        w_copy(k).wait_send()
    near_copy().wait_send()

    @pl.when(me == 0)
    def _():
        near_comp_copy().wait_send()
        for k in range(1, NS):
            near_comp_on(k).wait_send()

    for r in range(NS):
        g_copy(r, 0).wait_send()
        if r > 0:
            g_copy(r, 1).wait_send()

        @pl.when(r != me)
        def _():
            o_copy(r).wait_send()
            o_arrival(r).wait_recv()

    o_stay(me).wait()


def body(boundary, peps_rows, sketch, ranks, sizes, charges):
    any_space = pl.BlockSpec(memory_space=pl.ANY)
    smem = pl.BlockSpec(memory_space=pltpu.SMEM)
    vmem = pl.BlockSpec(memory_space=pltpu.VMEM)
    dma = pltpu.SemaphoreType.DMA
    result = pl.pallas_call(
        kernel,
        out_shape=pltpu.VMEM((NS, W * D, W), BF16),
        in_specs=[vmem, smem, smem, smem, any_space, any_space],
        out_specs=any_space,
        scratch_shapes=[
            pltpu.VMEM((NS, W * D, W), BF16),
            pltpu.VMEM((NS + 1, W * D, W), BF16),
            pltpu.VMEM((3, W * D, W), BF16),
            pltpu.VMEM((NS, W * D, W), BF16),
            pltpu.VMEM((NS, W * D, W), BF16),
            pltpu.VMEM((2, W, W * D), BF16),
            pltpu.VMEM((W, W * D), BF16),
            pltpu.VMEM((64, W), F32),
            pltpu.VMEM((NS, 64, W), BF16),
            pltpu.VMEM((3, 256, 256), BF16),
            pltpu.VMEM((2, W * D, W * D), BF16),
            pltpu.VMEM((W, W * D), F32),
            pltpu.VMEM((W * D, W), F32),
            pltpu.VMEM((2, W, W), F32),
            pltpu.VMEM((NS, 2, W, W), BF16),
            pltpu.VMEM((NS, 2, W, W), BF16),
            pltpu.VMEM((2, W, 2 * W), F32),
            pltpu.VMEM((2, W, W), F32),
            pltpu.VMEM((2, W, 4 * W), F32),
            pltpu.VMEM((HOPS, CHUNK, W), BF16),
            pltpu.VMEM((W * D, W), BF16),
            pltpu.VMEM((64, W), BF16),
            pltpu.VMEM((W * D, W), F32),
            dma((NS,)), dma(()), dma((NS - 1, CHUNKS)), dma((NS, CHUNKS)), dma((NS - 1,)),
            dma((NS,)), dma((NS, CHUNKS)), dma((NS, CHUNKS)), dma((NS, 2)), dma((NS, 2)),
            dma((NS,)), dma((NS,)), dma(()), dma((HOPS,)), dma((HOPS,)),
            dma((2,)), dma((2,)), dma((NS - 1,)),
        ],
        compiler_params=pltpu.CompilerParams(
            collective_id=0, has_side_effects=True, vmem_limit_bytes=56 * 2**20
        ),
        name="absorb_rows",
    )(
        peps_rows.reshape(D * D, D, D),
        ranks.reshape(NS),
        sizes,
        charges,
        boundary.reshape(NS, W * D, W),
        sketch.reshape(NS, W * D, W),
    )
    return result.reshape(1, 1, NS, W, D, W)


def solution(mesh):
    placed = (
        P("col", None, None, None, None),
        P("row", "col", None, None, None, None),
        P("row", "col", None, None, None),
        P("row", "col", None),
        P(),
        P(),
    )
    return jax.shard_map(
        body,
        mesh=mesh,
        in_specs=placed,
        out_specs=P("row", "col", None, None, None, None),
        check_vma=False,
    )
```

```python
import jax
import jax.numpy as jnp
from jax import lax
from jax.experimental import pallas as pl
from jax.experimental.pallas import tpu as pltpu
from jax.sharding import PartitionSpec as P

W = 128
D = 8
NS = 4
CHUNKS = 4
HOPS = 2
CHUNK = W * D // CHUNKS
F32 = jnp.float32
BF16 = jnp.bfloat16
MESH = pl.DeviceIdType.MESH


def iota(shape, axis):
    return lax.broadcasted_iota(jnp.int32, shape, axis)


def mm(a, b):
    return jnp.dot(a, b, preferred_element_type=F32)


def mm_nt(a, b):
    return lax.dot_general(a, b, (((1,), (1,)), ((), ())), preferred_element_type=F32)


def mm_tn(a, b):
    return lax.dot_general(a, b, (((0,), (0,)), ((), ())), preferred_element_type=F32)


def compact_tensor(peps_ref, charges_ref, compact):
    rows = iota((512, 1), 0)
    l, h, u = rows >> 6, (rows >> 3) & 7, rows & 7
    balance = jnp.zeros((512, 1), jnp.int32)
    for i in range(D):
        q = charges_ref[i]
        balance += q * (
            (l == i).astype(jnp.int32) + (u == i).astype(jnp.int32) - (h == i).astype(jnp.int32)
        )
    values = peps_ref[...].astype(F32).reshape(512, D)
    big = iota((512, W), 0)
    lane = iota((512, W), 1)
    from_row = jnp.where(lane < 64, big & 63, ((big >> 6) << 3) | (big & 7))
    same = from_row == (lane & 63)
    pick = iota((2 * D, 512), 0)
    source = iota((2 * D, 512), 1)
    wanted = jnp.where(pick < D, source >> 6, (source >> 3) & 7)
    picker = (wanted == (pick & 7)).astype(BF16)
    for d in range(D):
        column = jnp.where(balance == charges_ref[d], values[:, d : d + 1], 0.0)
        spread = jnp.where(same, jnp.broadcast_to(column, (512, W)), 0.0).astype(BF16)
        both = mm(picker, spread)
        compact[pl.ds(d * D, D), :] = jnp.where(iota((D, W), 1) < 64, both[:D], both[D:])


def halves(x):
    high = x.astype(BF16)
    return high, (x - high.astype(F32)).astype(BF16)


def mm3(a, b):
    ah, al = halves(a)
    bh, bl = halves(b)
    return mm(jnp.concatenate([ah, ah, al], axis=1), jnp.concatenate([bh, bl, bh], axis=0))


def mm3_tn(a, b):
    ah, al = halves(a)
    bh, bl = halves(b)
    return mm_tn(jnp.concatenate([ah, ah, al], axis=0), jnp.concatenate([bh, bl, bh], axis=0))


def vreg(x):
    return jnp.broadcast_to(x, (8, W))


def eliminate(tiles, beyond, first, part):
    sub = iota((8, W), 0)
    groups = [list(tiles)] + ([list(beyond)] if beyond else [])

    def spread(v, j):
        a, b = (first[0] + j) % W, (first[1] + j) % W
        return jnp.where(part, vreg(v[:, a : a + 1]), vreg(v[:, b : b + 1]))

    def row(x, i):
        return vreg(x[i : i + 1, :])

    tiles = groups[0]
    own = [spread(tiles[0], t) for t in range(8)]
    for q in range(4):
        low = {o: [spread(tiles[o], 8 * q + t) for t in range(8)] for o in range(q + 1, 4)}
        after = [spread(tiles[q + 1], 8 * q + 8 + t) for t in range(8)] if q < 3 else []
        pivots = None
        for t in range(0, 8, 2):
            one, cross, two = row(own[t], t), row(own[t], t + 1), row(own[t + 1], t + 1)
            determinant = one * two - cross * cross
            over_one = 1.0 / one
            over_two = one * (1.0 / determinant)
            ratio = cross * over_one
            schur = determinant * over_one
            pivots = one if t == 0 else jnp.where(sub == t, one, pivots)
            pivots = jnp.where(sub == t + 1, schur, pivots)
            rows_one = {k: row(own[t], k) for k in range(t + 2, 8)}
            rows_two = {k: row(own[t + 1], k) - ratio * rows_one[k] for k in range(t + 2, 8)}
            factor_one = own[t] * over_one
            factor_two = (own[t + 1] - own[t] * ratio) * over_two
            for k in range(t + 2, 8):
                own[k] = (own[k] - factor_one * rows_one[k]) - factor_two * rows_two[k]
            factor_one = jnp.where(sub > t, factor_one, 0.0)
            factor_two = jnp.where(sub > t + 1, factor_two, 0.0)
            here = []
            for group in groups:
                upper = row(group[q], t)
                here.append((upper, row(group[q], t + 1) - ratio * upper))
            for o in range(q + 1, 4):
                second = low[o][t + 1] - low[o][t] * ratio
                below_one = low[o][t] * over_one
                below_two = second * over_two
                if o == q + 1:
                    for k in range(8):
                        after[k] = (after[k] - below_one * row(low[o][t], k)) - below_two * row(
                            second, k
                        )
                for k in range(t + 2, 8):
                    low[o][k] = (low[o][k] - below_one * rows_one[k]) - below_two * rows_two[k]
                for group, (upper, lower) in zip(groups, here):
                    group[o] = (group[o] - below_one * upper) - below_two * lower
            for group, (upper, lower) in zip(groups, here):
                group[q] = (group[q] - factor_one * upper) - factor_two * lower
        root = lax.rsqrt(pivots)
        for group in groups:
            group[q] = group[q] * root
        own = after
    return groups


def inverse_factors(work, inverse, mixed):
    lane, sub = iota((8, W), 1), iota((8, W), 0)
    group = lane >> 5
    ready = None
    for k in range(4):
        at = [(k + i) % 4 for i in range(4)]
        part = (group == at[0]) | (group == at[1])
        tiles, beyond = [], []
        for q in range(4):
            rows = pl.ds(32 * k + 8 * q, 8)
            one, two = work[0, rows, :W], pltpu.roll(work[1, rows, :W], 64, 1)
            if k < 3:
                beyond.append(jnp.where(group == at[1], one, jnp.where(group == at[3], two, 0.0)))
            if k > 0:
                one, two = ready[q]
            unit = ((lane & 31) == (sub + 8 * q)).astype(F32)
            tiles.append(jnp.where(group == at[0], one, jnp.where(group == at[2], two, unit)))
        done = eliminate(tiles, beyond, (32 * k, 32 * k + 64), part)
        if k < 3:
            ahead = jnp.concatenate(done[1], axis=0)
            update = mm3_tn(ahead, ahead)
            ready = []
            for q in range(4):
                rows = pl.ds(32 * (k + 1) + 8 * q, 8)
                one = work[0, rows, :W] - update[32 * at[1] + 8 * q : 32 * at[1] + 8 * q + 8]
                two = pltpu.roll(work[1, rows, :W], 64, 1)
                ready.append((one, two - update[32 * at[3] + 8 * q : 32 * at[3] + 8 * q + 8]))
        slot = k % 2
        mixed[slot] = jnp.zeros((W, 4 * W), F32)
        mixed[slot, pl.ds(32 * at[1], 32), : 2 * W] = work[0, pl.ds(32 * k, 32), :]
        mixed[slot, pl.ds(32 * at[3], 32), 2 * W :] = work[1, pl.ds(32 * k, 32), :]
        both = mm3(jnp.concatenate(done[0], axis=0), mixed[slot])
        for i in range(2):
            panel = both[:, i * 2 * W : (i + 1) * 2 * W]
            inverse[i, pl.ds(32 * k, 32), :] = panel[:, W:]
            if k < 3:
                below = 32 * (k + 1)
                update = mm3_tn(panel[:, :W], panel)
                work[i, pl.ds(below, W - below), :] -= update[below:, :]


def kernel(
    peps_ref, ranks_ref, sizes_ref, charges_ref, boundary_ref, sketch_ref, out_ref,
    sk, bm, sides, r_raw, l_raw, wides, l_turned, comp32, comp, kron, z, mid, tall,
    gram_own, gram_out, gram_in, work, inverse, mixed, hop, near, near_comp, turned,
    sk_sem, b_sem, r_send, r_recv, w_send, w_recv, l_send, l_recv,
    g_send, g_recv, o_send, o_recv, o_local, hop_recv, hop_send,
    near_send, near_recv, near_on,
):
    me = lax.axis_index("row")
    col = lax.axis_index("col")
    cols = lax.axis_size("col")
    right = lax.rem(col + 1, cols)
    left = lax.rem(col + cols - 1, cols)

    def sketch_load(s):
        return pltpu.make_async_copy(sketch_ref.at[s], sk.at[s], sk_sem.at[s])

    def chunk(c):
        return pl.ds(c * CHUNK, CHUNK)

    def r_copy(k, c):
        s = lax.rem(me + k, NS)
        return pltpu.make_async_remote_copy(
            src_ref=sk.at[s, chunk(c)], dst_ref=r_raw.at[me, chunk(c)],
            send_sem=r_send.at[k - 1, c], recv_sem=r_recv.at[me, c],
            device_id=(s, col), device_id_type=MESH,
        )

    def r_arrival(r, c):
        return pltpu.make_async_remote_copy(
            src_ref=sk.at[0, chunk(c)], dst_ref=r_raw.at[r, chunk(c)],
            send_sem=r_send.at[0, c], recv_sem=r_recv.at[r, c],
            device_id=(me, col), device_id_type=MESH,
        )

    def l_copy(r, c):
        return pltpu.make_async_remote_copy(
            src_ref=r_raw.at[r, chunk(c)], dst_ref=l_raw.at[r, chunk(c)],
            send_sem=l_send.at[r, c], recv_sem=l_recv.at[r, c],
            device_id=(me, right), device_id_type=MESH,
        )

    def w_copy(k):
        s = lax.rem(me + k, NS)
        return pltpu.make_async_remote_copy(
            src_ref=comp.at[me], dst_ref=comp.at[me], send_sem=w_send.at[k - 1],
            recv_sem=w_recv.at[me], device_id=(s, col), device_id_type=MESH,
        )

    def w_arrival(r):
        return pltpu.make_async_remote_copy(
            src_ref=comp.at[r], dst_ref=comp.at[r], send_sem=w_send.at[0],
            recv_sem=w_recv.at[r], device_id=(me, col), device_id_type=MESH,
        )

    def g_copy(r, side):
        return pltpu.make_async_remote_copy(
            src_ref=gram_out.at[r, side], dst_ref=gram_in.at[r, side],
            send_sem=g_send.at[r, side], recv_sem=g_recv.at[r, side],
            device_id=(me, right + side * (left - right)), device_id_type=MESH,
        )

    def o_copy(r):
        return pltpu.make_async_remote_copy(
            src_ref=bm.at[r + 1], dst_ref=out_ref.at[me], send_sem=o_send.at[r],
            recv_sem=o_recv.at[me], device_id=(r, col), device_id_type=MESH,
        )

    def o_arrival(s):
        return pltpu.make_async_remote_copy(
            src_ref=bm.at[1], dst_ref=out_ref.at[s], send_sem=o_send.at[0],
            recv_sem=o_recv.at[s], device_id=(me, col), device_id_type=MESH,
        )

    def o_stay(r):
        return pltpu.make_async_copy(bm.at[r + 1], out_ref.at[me], o_local)

    def hop_in(c):
        return pltpu.make_async_remote_copy(
            src_ref=sk.at[2, chunk(c)], dst_ref=hop.at[c], send_sem=r_send.at[1, c],
            recv_sem=hop_recv.at[c], device_id=(3, col), device_id_type=MESH,
        )

    def hop_on(c):
        return pltpu.make_async_remote_copy(
            src_ref=hop.at[c], dst_ref=r_raw.at[0, chunk(c)], send_sem=hop_send.at[c],
            recv_sem=r_recv.at[0, c], device_id=(2, col), device_id_type=MESH,
        )

    def near_copy():
        return pltpu.make_async_remote_copy(
            src_ref=bm.at[0], dst_ref=near, send_sem=near_send.at[0], recv_sem=near_recv.at[0],
            device_id=(me, left), device_id_type=MESH,
        )

    def near_comp_copy():
        return pltpu.make_async_remote_copy(
            src_ref=comp.at[0], dst_ref=near_comp, send_sem=near_send.at[1],
            recv_sem=near_recv.at[1], device_id=(me, left), device_id_type=MESH,
        )

    def near_comp_on(k):
        return pltpu.make_async_remote_copy(
            src_ref=near_comp, dst_ref=near_comp, send_sem=near_on.at[k - 1],
            recv_sem=near_recv.at[1], device_id=(k, col), device_id_type=MESH,
        )

    def send_result(r):
        @pl.when(r != me)
        def _():
            o_copy(r).start()

        @pl.when(r == me)
        def _():
            o_stay(r).start()

    def send_sketch(k):
        for c in range(CHUNKS):
            r_copy(k, c).start()

    barrier = pltpu.get_barrier_semaphore()
    for k in range(1, NS):
        pl.semaphore_signal(
            barrier, inc=1, device_id=(lax.rem(me + k, NS), col), device_id_type=MESH
        )
    for c in (left, right):
        pl.semaphore_signal(barrier, inc=1, device_id=(me, c), device_id_type=MESH)
    away = [lax.rem(me + k, NS) for k in (1, 2, 3, 0)]
    for s in away:
        sketch_load(s).start()
    boundary_load = pltpu.make_async_copy(boundary_ref.at[me], bm.at[0], b_sem)
    boundary_load.start()
    lanes = iota((1, W), 1)

    def mask_sketch(s):
        sketch_load(s).wait()
        sk[s] = sk[s] * (lanes < ranks_ref[s]).astype(BF16)

    mask_sketch(away[0])
    mask_sketch(away[1])
    pl.semaphore_wait(barrier, NS + 1)

    @pl.when(me == 0)
    def _():
        send_sketch(1)
        for c in range(HOPS):
            hop_in(c).start()

    mask_sketch(away[2])
    mask_sketch(away[3])
    r_raw[me] = sk[me]

    @pl.when(me == 1)
    def _():
        send_sketch(3)

    @pl.when(me == 2)
    def _():
        send_sketch(1)
        send_sketch(3)
        send_sketch(2)

    boundary_load.wait()
    near_copy().start()
    compact_tensor(peps_ref, charges_ref, comp32)
    comp[me] = comp32[...].astype(BF16)

    @pl.when(me == 0)
    def _():
        near_comp_copy().start()

    for k in range(1, NS):
        w_copy(k).start()

    block = iota((256, 256), 0) >> 6 == iota((256, 256), 1) >> 6

    def relay(r):
        for c in range(CHUNKS):

            @pl.when(r != me)
            def _():
                r_arrival(r, c).wait_recv()

            l_copy(r, c).start()

        @pl.when(r != me)
        def _():
            w_arrival(r).wait_recv()

    def regroup(side, natural):
        tall[...] = natural
        for h in range(D):
            wides[side, :, h * W : (h + 1) * W] = tall[pl.ds(h, W, stride=D), :].astype(BF16)

    def expand(both, slots):
        rolled = pltpu.roll(both, 64, 1)
        low = iota((64, W), 1) < 64
        for i, slot in slots:
            twice = jnp.where(low, both, rolled) if i == 0 else jnp.where(low, rolled, both)
            four = jnp.concatenate([twice, twice], axis=1)
            kron[slot] = jnp.where(block, jnp.concatenate([four] * 4, axis=0), 0.0).astype(BF16)

    def prepare_right(r):
        regroup(0, r_raw[r].astype(F32))
        expand(comp[r].astype(F32), ((0, 0), (1, 1)))

    def prepare_left(r):
        natural = l_raw[r].astype(F32)
        regroup(1, natural)
        l_turned[...] = natural.T.astype(BF16)

    def left_arrives(r):
        for c in range(CHUNKS):
            l_copy(r, c).wait_recv()

    def absorb_side(lhs, wide, side):
        part = mm(sides[lhs], wides[wide])
        columns = []
        for q in range(W // 4):
            pieces = [
                part[(4 * q + i) * D : (4 * q + i + 1) * D, h * W : (h + 1) * W]
                for i in range(4)
                for h in range(D)
            ]
            columns.append(jnp.concatenate(pieces, axis=0).astype(BF16))
        whole = mm(kron[lhs], jnp.concatenate(columns, axis=1))
        for d in range(D):
            pieces = [
                whole[(i * D + d) * D : (i * D + d + 1) * D, q * W : (q + 1) * W]
                for q in range(W // 4)
                for i in range(4)
            ]
            z[side, :, d * W : (d + 1) * W] = jnp.concatenate(pieces, axis=0).astype(BF16)
        gram = jnp.zeros((W, W), F32)
        for d in range(D):
            piece = z[side, :, d * W : (d + 1) * W]
            gram += mm_tn(piece, piece)
        gram_own[side] = gram

    def send_gram(r, side):
        gram_out[r, side] = gram_own[side].astype(BF16)
        g_copy(r, side).start()

    def masked(block):
        size = sizes_ref[me]
        inside = ((iota((W * D, W), 0) >> 3) < size) & (iota((W * D, W), 1) < size)
        return jnp.where(inside, block.astype(F32), 0.0)

    def turn_side(start, side):
        tall[...] = start
        for u in range(D):
            mid[:, u * W : (u + 1) * W] = tall[pl.ds(u, W, stride=D), :].T
        for u in range(D):
            tall[pl.ds(u, W, stride=D), :] = mid[:, u * W : (u + 1) * W]
        sides[side] = tall[...].astype(BF16)

    def prepare_near():
        near_copy().wait_recv()
        turn_side(masked(near[...]), 2)

    sides[0] = masked(bm[0]).astype(BF16)

    @pl.when(me != 0)
    def _():
        prepare_near()

    @pl.when(me == 3)
    def _():
        for c in range(HOPS):
            hop_in(c).wait_recv()
            hop_on(c).start()

    relay(0)
    prepare_right(0)

    @pl.when(me == 1)
    def _():
        send_sketch(1)

    eye = (iota((W, W), 0) == iota((W, W), 1)).astype(F32)

    def absorb(r, carry):
        first_row = r == 0
        early = jnp.where(first_row, 0, 1 - lax.rem(col, 2))
        absorb_side(early, early, early)

        @pl.when(first_row)
        def _():
            @pl.when(me == 0)
            def _():
                for c in range(HOPS):
                    hop_in(c).wait_send()
                send_sketch(3)
                for c in range(CHUNKS):
                    r_copy(1, c).wait_send()
                for c in range(HOPS, CHUNKS):
                    r_copy(2, c).start()
                near_comp_copy().wait_recv()
                for k in range(1, NS):
                    near_comp_on(k).start()
                prepare_near()

            @pl.when(me != 0)
            def _():
                near_comp_copy().wait_recv()

            expand(near_comp[...].astype(F32), ((1, 2),))

        @pl.when(jnp.logical_not(first_row))
        def _():
            send_gram(r, early)

        absorb_side(
            jnp.where(first_row, 2, 1 - early), jnp.where(first_row, 0, 1 - early), 1 - early
        )

        @pl.when(first_row)
        def _():
            gram_out[0, 0] = (gram_own[0] + gram_own[1]).astype(BF16)
            g_copy(0, 0).start()
            gram_in[0, 1] = gram_own[1].astype(BF16)
            gram_own[1] = jnp.zeros((W, W), F32)

            left_arrives(0)
            l_turned[...] = l_raw[0].astype(F32).T.astype(BF16)

        @pl.when(jnp.logical_not(first_row))
        def _():
            send_gram(r, 1 - early)

        mid[...] = mm(l_turned[...], z[0])

        @pl.when((r == 0) & (me == 1))
        def _():
            send_sketch(2)

        @pl.when((r == 0) & (me == 3))
        def _():
            for k in range(1, NS):
                send_sketch(k)

        @pl.when(r == 0)
        def _():
            relay(1)
            prepare_right(1)

        @pl.when((r > 0) & (r < NS - 1))
        def _():
            left_arrives(r + 1)
            prepare_left(r + 1)
            prepare_right(r + 1)

        g_copy(r, 0).wait_recv()

        @pl.when(r > 0)
        def _():
            g_copy(r, 1).wait_recv()

        for side in range(2):
            work[side, :, :W] = gram_in[r, side].astype(F32) + gram_own[1 - side] + eye
            work[side, :, W:] = eye
        inverse_factors(work, inverse, mixed)

        @pl.when(r < NS - 2)
        def _():
            relay(r + 2)

        @pl.when(r == 0)
        def _():
            left_arrives(1)
            prepare_left(1)

        def solved():
            lefted = mm3(inverse[0], mid[...])
            for d in range(D):
                tall[pl.ds(d, W, stride=D), :] = lefted[:, d * W : (d + 1) * W]
            high, low = halves(inverse[1])
            second = jnp.concatenate([high, low, high], axis=1)
            high, low = halves(tall[...])
            fresh = mm_nt(jnp.concatenate([high, high, low], axis=1), second)
            return lefted, second, fresh, lax.rsqrt(jnp.mean(fresh * fresh) + 1e-6)

        @pl.when(r < NS - 1)
        def _():
            lefted, second, fresh, scaling = solved()
            high, low = halves(lefted)
            for d in range(D):
                lanes_d = slice(d * W, (d + 1) * W)
                piece = jnp.concatenate([high[:, lanes_d], high[:, lanes_d], low[:, lanes_d]], axis=1)
                turned[pl.ds(d, W, stride=D), :] = mm_nt(second, piece)
            result = (fresh * scaling).astype(BF16)
            sides[0] = result
            bm[r + 1] = result
            sides[1] = (turned[...] * scaling).astype(BF16)
            send_result(r)

        @pl.when(r == NS - 1)
        def _():
            _, _, fresh, scaling = solved()
            bm[r + 1] = (fresh * scaling).astype(BF16)
            send_result(r)

        return carry

    lax.fori_loop(0, NS, absorb, 0)

    for c in range(CHUNKS):

        @pl.when(me != 0)
        def _():
            r_copy(1, c).wait_send()

        if c < HOPS:

            @pl.when(me != 0)
            def _():
                r_copy(2, c).wait_send()

            @pl.when(me == 3)
            def _():
                hop_on(c).wait_send()

        else:
            r_copy(2, c).wait_send()
        r_copy(3, c).wait_send()
        for r in range(NS):
            l_copy(r, c).wait_send()
    for k in range(1, NS):
        w_copy(k).wait_send()
    near_copy().wait_send()

    @pl.when(me == 0)
    def _():
        near_comp_copy().wait_send()
        for k in range(1, NS):
            near_comp_on(k).wait_send()

    for r in range(NS):
        g_copy(r, 0).wait_send()
        if r > 0:
            g_copy(r, 1).wait_send()

        @pl.when(r != me)
        def _():
            o_copy(r).wait_send()
            o_arrival(r).wait_recv()

    o_stay(me).wait()


def body(boundary, peps_rows, sketch, ranks, sizes, charges):
    any_space = pl.BlockSpec(memory_space=pl.ANY)
    smem = pl.BlockSpec(memory_space=pltpu.SMEM)
    vmem = pl.BlockSpec(memory_space=pltpu.VMEM)
    dma = pltpu.SemaphoreType.DMA
    result = pl.pallas_call(
        kernel,
        out_shape=pltpu.VMEM((NS, W * D, W), BF16),
        in_specs=[vmem, smem, smem, smem, any_space, any_space],
        out_specs=any_space,
        scratch_shapes=[
            pltpu.VMEM((NS, W * D, W), BF16),
            pltpu.VMEM((NS + 1, W * D, W), BF16),
            pltpu.VMEM((3, W * D, W), BF16),
            pltpu.VMEM((NS, W * D, W), BF16),
            pltpu.VMEM((NS, W * D, W), BF16),
            pltpu.VMEM((2, W, W * D), BF16),
            pltpu.VMEM((W, W * D), BF16),
            pltpu.VMEM((64, W), F32),
            pltpu.VMEM((NS, 64, W), BF16),
            pltpu.VMEM((3, 256, 256), BF16),
            pltpu.VMEM((2, W * D, W * D), BF16),
            pltpu.VMEM((W, W * D), F32),
            pltpu.VMEM((W * D, W), F32),
            pltpu.VMEM((2, W, W), F32),
            pltpu.VMEM((NS, 2, W, W), BF16),
            pltpu.VMEM((NS, 2, W, W), BF16),
            pltpu.VMEM((2, W, 2 * W), F32),
            pltpu.VMEM((2, W, W), F32),
            pltpu.VMEM((2, W, 4 * W), F32),
            pltpu.VMEM((HOPS, CHUNK, W), BF16),
            pltpu.VMEM((W * D, W), BF16),
            pltpu.VMEM((64, W), BF16),
            pltpu.VMEM((W * D, W), F32),
            dma((NS,)), dma(()), dma((NS - 1, CHUNKS)), dma((NS, CHUNKS)), dma((NS - 1,)),
            dma((NS,)), dma((NS, CHUNKS)), dma((NS, CHUNKS)), dma((NS, 2)), dma((NS, 2)),
            dma((NS,)), dma((NS,)), dma(()), dma((HOPS,)), dma((HOPS,)),
            dma((2,)), dma((2,)), dma((NS - 1,)),
        ],
        compiler_params=pltpu.CompilerParams(
            collective_id=0, has_side_effects=True, vmem_limit_bytes=56 * 2**20
        ),
        name="absorb_rows",
    )(
        peps_rows.reshape(D * D, D, D),
        ranks.reshape(NS),
        sizes,
        charges,
        boundary.reshape(NS, W * D, W),
        sketch.reshape(NS, W * D, W),
    )
    return result.reshape(1, 1, NS, W, D, W)


def solution(mesh):
    placed = (
        P("col", None, None, None, None),
        P("row", "col", None, None, None, None),
        P("row", "col", None, None, None),
        P("row", "col", None),
        P(),
        P(),
    )
    return jax.shard_map(
        body,
        mesh=mesh,
        in_specs=placed,
        out_specs=P("row", "col", None, None, None, None),
        check_vma=False,
    )
```

```python
import jax
import jax.numpy as jnp
from jax import lax
from jax.experimental import pallas as pl
from jax.experimental.pallas import tpu as pltpu
from jax.sharding import PartitionSpec as P

W = 128
D = 8
NS = 4
CHUNKS = 2
HOPS = 1
CHUNK = W * D // CHUNKS
F32 = jnp.float32
BF16 = jnp.bfloat16
MESH = pl.DeviceIdType.MESH


def iota(shape, axis):
    return lax.broadcasted_iota(jnp.int32, shape, axis)


def mm(a, b):
    return jnp.dot(a, b, preferred_element_type=F32)


def mm_nt(a, b):
    return lax.dot_general(a, b, (((1,), (1,)), ((), ())), preferred_element_type=F32)


def mm_tn(a, b):
    return lax.dot_general(a, b, (((0,), (0,)), ((), ())), preferred_element_type=F32)


def compact_tensor(peps_ref, charges_ref, compact):
    rows = iota((512, 1), 0)
    l, h, u = rows >> 6, (rows >> 3) & 7, rows & 7
    balance = jnp.zeros((512, 1), jnp.int32)
    for i in range(D):
        q = charges_ref[i]
        balance += q * (
            (l == i).astype(jnp.int32) + (u == i).astype(jnp.int32) - (h == i).astype(jnp.int32)
        )
    values = peps_ref[...].astype(F32).reshape(512, D)
    big = iota((512, W), 0)
    lane = iota((512, W), 1)
    from_row = jnp.where(lane < 64, big & 63, ((big >> 6) << 3) | (big & 7))
    same = from_row == (lane & 63)
    pick = iota((2 * D, 512), 0)
    source = iota((2 * D, 512), 1)
    wanted = jnp.where(pick < D, source >> 6, (source >> 3) & 7)
    picker = (wanted == (pick & 7)).astype(BF16)
    for d in range(D):
        column = jnp.where(balance == charges_ref[d], values[:, d : d + 1], 0.0)
        spread = jnp.where(same, jnp.broadcast_to(column, (512, W)), 0.0).astype(BF16)
        both = mm(picker, spread)
        compact[pl.ds(d * D, D), :] = jnp.where(iota((D, W), 1) < 64, both[:D], both[D:])


def halves(x):
    high = x.astype(BF16)
    return high, (x - high.astype(F32)).astype(BF16)


def mm3(a, b):
    ah, al = halves(a)
    bh, bl = halves(b)
    return mm(jnp.concatenate([ah, ah, al], axis=1), jnp.concatenate([bh, bl, bh], axis=0))


def mm3_tn(a, b):
    ah, al = halves(a)
    bh, bl = halves(b)
    return mm_tn(jnp.concatenate([ah, ah, al], axis=0), jnp.concatenate([bh, bl, bh], axis=0))


def vreg(x):
    return jnp.broadcast_to(x, (8, W))


def eliminate(tiles, beyond, first, part):
    sub = iota((8, W), 0)
    groups = [list(tiles)] + ([list(beyond)] if beyond else [])

    def spread(v, j):
        a, b = (first[0] + j) % W, (first[1] + j) % W
        return jnp.where(part, vreg(v[:, a : a + 1]), vreg(v[:, b : b + 1]))

    def row(x, i):
        return vreg(x[i : i + 1, :])

    tiles = groups[0]
    own = [spread(tiles[0], t) for t in range(8)]
    for q in range(4):
        low = {o: [spread(tiles[o], 8 * q + t) for t in range(8)] for o in range(q + 1, 4)}
        after = [spread(tiles[q + 1], 8 * q + 8 + t) for t in range(8)] if q < 3 else []
        pivots = None
        for t in range(0, 8, 2):
            one, cross, two = row(own[t], t), row(own[t], t + 1), row(own[t + 1], t + 1)
            determinant = one * two - cross * cross
            over_one = 1.0 / one
            over_two = one * (1.0 / determinant)
            ratio = cross * over_one
            schur = determinant * over_one
            pivots = one if t == 0 else jnp.where(sub == t, one, pivots)
            pivots = jnp.where(sub == t + 1, schur, pivots)
            rows_one = {k: row(own[t], k) for k in range(t + 2, 8)}
            rows_two = {k: row(own[t + 1], k) - ratio * rows_one[k] for k in range(t + 2, 8)}
            factor_one = own[t] * over_one
            factor_two = (own[t + 1] - own[t] * ratio) * over_two
            for k in range(t + 2, 8):
                own[k] = (own[k] - factor_one * rows_one[k]) - factor_two * rows_two[k]
            factor_one = jnp.where(sub > t, factor_one, 0.0)
            factor_two = jnp.where(sub > t + 1, factor_two, 0.0)
            here = []
            for group in groups:
                upper = row(group[q], t)
                here.append((upper, row(group[q], t + 1) - ratio * upper))
            for o in range(q + 1, 4):
                second = low[o][t + 1] - low[o][t] * ratio
                below_one = low[o][t] * over_one
                below_two = second * over_two
                if o == q + 1:
                    for k in range(8):
                        after[k] = (after[k] - below_one * row(low[o][t], k)) - below_two * row(
                            second, k
                        )
                for k in range(t + 2, 8):
                    low[o][k] = (low[o][k] - below_one * rows_one[k]) - below_two * rows_two[k]
                for group, (upper, lower) in zip(groups, here):
                    group[o] = (group[o] - below_one * upper) - below_two * lower
            for group, (upper, lower) in zip(groups, here):
                group[q] = (group[q] - factor_one * upper) - factor_two * lower
        root = lax.rsqrt(pivots)
        for group in groups:
            group[q] = group[q] * root
        own = after
    return groups


def inverse_factors(work, inverse, mixed):
    lane, sub = iota((8, W), 1), iota((8, W), 0)
    group = lane >> 5
    ready = None
    for k in range(4):
        at = [(k + i) % 4 for i in range(4)]
        part = (group == at[0]) | (group == at[1])
        tiles, beyond = [], []
        for q in range(4):
            rows = pl.ds(32 * k + 8 * q, 8)
            one, two = work[0, rows, :W], pltpu.roll(work[1, rows, :W], 64, 1)
            if k < 3:
                beyond.append(jnp.where(group == at[1], one, jnp.where(group == at[3], two, 0.0)))
            if k > 0:
                one, two = ready[q]
            unit = ((lane & 31) == (sub + 8 * q)).astype(F32)
            tiles.append(jnp.where(group == at[0], one, jnp.where(group == at[2], two, unit)))
        done = eliminate(tiles, beyond, (32 * k, 32 * k + 64), part)
        if k < 3:
            ahead = jnp.concatenate(done[1], axis=0)
            update = mm3_tn(ahead, ahead)
            ready = []
            for q in range(4):
                rows = pl.ds(32 * (k + 1) + 8 * q, 8)
                one = work[0, rows, :W] - update[32 * at[1] + 8 * q : 32 * at[1] + 8 * q + 8]
                two = pltpu.roll(work[1, rows, :W], 64, 1)
                ready.append((one, two - update[32 * at[3] + 8 * q : 32 * at[3] + 8 * q + 8]))
        slot = k % 2
        mixed[slot] = jnp.zeros((W, 4 * W), F32)
        mixed[slot, pl.ds(32 * at[1], 32), : 2 * W] = work[0, pl.ds(32 * k, 32), :]
        mixed[slot, pl.ds(32 * at[3], 32), 2 * W :] = work[1, pl.ds(32 * k, 32), :]
        both = mm3(jnp.concatenate(done[0], axis=0), mixed[slot])
        for i in range(2):
            panel = both[:, i * 2 * W : (i + 1) * 2 * W]
            inverse[i, pl.ds(32 * k, 32), :] = panel[:, W:]
            if k < 3:
                below = 32 * (k + 1)
                update = mm3_tn(panel[:, :W], panel)
                work[i, pl.ds(below, W - below), :] -= update[below:, :]


def kernel(
    peps_ref, ranks_ref, sizes_ref, charges_ref, boundary_ref, sketch_ref, out_ref,
    sk, bm, sides, r_raw, l_raw, wides, l_turned, comp32, comp, kron, z, mid, tall,
    gram_own, gram_out, gram_in, work, inverse, mixed, hop, near, near_comp, turned,
    sk_sem, b_sem, r_send, r_recv, w_send, w_recv, l_send, l_recv,
    g_send, g_recv, o_send, o_recv, o_local, hop_recv, hop_send,
    near_send, near_recv, near_on,
):
    me = lax.axis_index("row")
    col = lax.axis_index("col")
    cols = lax.axis_size("col")
    right = lax.rem(col + 1, cols)
    left = lax.rem(col + cols - 1, cols)

    def sketch_load(s):
        return pltpu.make_async_copy(sketch_ref.at[s], sk.at[s], sk_sem.at[s])

    def chunk(c):
        return pl.ds(c * CHUNK, CHUNK)

    def r_copy(k, c):
        s = lax.rem(me + k, NS)
        return pltpu.make_async_remote_copy(
            src_ref=sk.at[s, chunk(c)], dst_ref=r_raw.at[me, chunk(c)],
            send_sem=r_send.at[k - 1, c], recv_sem=r_recv.at[me, c],
            device_id=(s, col), device_id_type=MESH,
        )

    def r_arrival(r, c):
        return pltpu.make_async_remote_copy(
            src_ref=sk.at[0, chunk(c)], dst_ref=r_raw.at[r, chunk(c)],
            send_sem=r_send.at[0, c], recv_sem=r_recv.at[r, c],
            device_id=(me, col), device_id_type=MESH,
        )

    def l_copy(r, c):
        return pltpu.make_async_remote_copy(
            src_ref=r_raw.at[r, chunk(c)], dst_ref=l_raw.at[r, chunk(c)],
            send_sem=l_send.at[r, c], recv_sem=l_recv.at[r, c],
            device_id=(me, right), device_id_type=MESH,
        )

    def w_copy(k):
        s = lax.rem(me + k, NS)
        return pltpu.make_async_remote_copy(
            src_ref=comp.at[me], dst_ref=comp.at[me], send_sem=w_send.at[k - 1],
            recv_sem=w_recv.at[me], device_id=(s, col), device_id_type=MESH,
        )

    def w_arrival(r):
        return pltpu.make_async_remote_copy(
            src_ref=comp.at[r], dst_ref=comp.at[r], send_sem=w_send.at[0],
            recv_sem=w_recv.at[r], device_id=(me, col), device_id_type=MESH,
        )

    def g_copy(r, side):
        return pltpu.make_async_remote_copy(
            src_ref=gram_out.at[r, side], dst_ref=gram_in.at[r, side],
            send_sem=g_send.at[r, side], recv_sem=g_recv.at[r, side],
            device_id=(me, right + side * (left - right)), device_id_type=MESH,
        )

    def o_copy(r):
        return pltpu.make_async_remote_copy(
            src_ref=bm.at[r + 1], dst_ref=out_ref.at[me], send_sem=o_send.at[r],
            recv_sem=o_recv.at[me], device_id=(r, col), device_id_type=MESH,
        )

    def o_arrival(s):
        return pltpu.make_async_remote_copy(
            src_ref=bm.at[1], dst_ref=out_ref.at[s], send_sem=o_send.at[0],
            recv_sem=o_recv.at[s], device_id=(me, col), device_id_type=MESH,
        )

    def o_stay(r):
        return pltpu.make_async_copy(bm.at[r + 1], out_ref.at[me], o_local)

    def hop_in(c):
        return pltpu.make_async_remote_copy(
            src_ref=sk.at[2, chunk(c)], dst_ref=hop.at[c], send_sem=r_send.at[1, c],
            recv_sem=hop_recv.at[c], device_id=(3, col), device_id_type=MESH,
        )

    def hop_on(c):
        return pltpu.make_async_remote_copy(
            src_ref=hop.at[c], dst_ref=r_raw.at[0, chunk(c)], send_sem=hop_send.at[c],
            recv_sem=r_recv.at[0, c], device_id=(2, col), device_id_type=MESH,
        )

    def near_copy():
        return pltpu.make_async_remote_copy(
            src_ref=bm.at[0], dst_ref=near, send_sem=near_send.at[0], recv_sem=near_recv.at[0],
            device_id=(me, left), device_id_type=MESH,
        )

    def near_comp_copy():
        return pltpu.make_async_remote_copy(
            src_ref=comp.at[0], dst_ref=near_comp, send_sem=near_send.at[1],
            recv_sem=near_recv.at[1], device_id=(me, left), device_id_type=MESH,
        )

    def near_comp_on(k):
        return pltpu.make_async_remote_copy(
            src_ref=near_comp, dst_ref=near_comp, send_sem=near_on.at[k - 1],
            recv_sem=near_recv.at[1], device_id=(k, col), device_id_type=MESH,
        )

    def send_result(r):
        @pl.when(r != me)
        def _():
            o_copy(r).start()

        @pl.when(r == me)
        def _():
            o_stay(r).start()

    def send_sketch(k):
        for c in range(CHUNKS):
            r_copy(k, c).start()

    barrier = pltpu.get_barrier_semaphore()
    for k in range(1, NS):
        pl.semaphore_signal(
            barrier, inc=1, device_id=(lax.rem(me + k, NS), col), device_id_type=MESH
        )
    for c in (left, right):
        pl.semaphore_signal(barrier, inc=1, device_id=(me, c), device_id_type=MESH)
    away = [lax.rem(me + k, NS) for k in (1, 2, 3, 0)]
    for s in away:
        sketch_load(s).start()
    boundary_load = pltpu.make_async_copy(boundary_ref.at[me], bm.at[0], b_sem)
    boundary_load.start()
    lanes = iota((1, W), 1)

    def mask_sketch(s):
        sketch_load(s).wait()
        sk[s] = sk[s] * (lanes < ranks_ref[s]).astype(BF16)

    mask_sketch(away[0])
    mask_sketch(away[1])
    pl.semaphore_wait(barrier, NS + 1)

    @pl.when(me == 0)
    def _():
        send_sketch(1)
        for c in range(HOPS):
            hop_in(c).start()

    mask_sketch(away[2])
    mask_sketch(away[3])
    r_raw[me] = sk[me]

    @pl.when(me == 1)
    def _():
        send_sketch(3)

    @pl.when(me == 2)
    def _():
        send_sketch(1)
        send_sketch(3)
        send_sketch(2)

    boundary_load.wait()
    near_copy().start()
    compact_tensor(peps_ref, charges_ref, comp32)
    comp[me] = comp32[...].astype(BF16)

    @pl.when(me == 0)
    def _():
        near_comp_copy().start()

    for k in range(1, NS):
        w_copy(k).start()

    block = iota((256, 256), 0) >> 6 == iota((256, 256), 1) >> 6

    def relay(r):
        for c in range(CHUNKS):

            @pl.when(r != me)
            def _():
                r_arrival(r, c).wait_recv()

            l_copy(r, c).start()

        @pl.when(r != me)
        def _():
            w_arrival(r).wait_recv()

    def regroup(side, natural):
        tall[...] = natural
        for h in range(D):
            wides[side, :, h * W : (h + 1) * W] = tall[pl.ds(h, W, stride=D), :].astype(BF16)

    def expand(both, slots):
        rolled = pltpu.roll(both, 64, 1)
        low = iota((64, W), 1) < 64
        for i, slot in slots:
            twice = jnp.where(low, both, rolled) if i == 0 else jnp.where(low, rolled, both)
            four = jnp.concatenate([twice, twice], axis=1)
            kron[slot] = jnp.where(block, jnp.concatenate([four] * 4, axis=0), 0.0).astype(BF16)

    def prepare_right(r):
        regroup(0, r_raw[r].astype(F32))
        expand(comp[r].astype(F32), ((0, 0), (1, 1)))

    def prepare_left(r):
        natural = l_raw[r].astype(F32)
        regroup(1, natural)
        l_turned[...] = natural.T.astype(BF16)

    def left_arrives(r):
        for c in range(CHUNKS):
            l_copy(r, c).wait_recv()

    def absorb_side(lhs, wide, side):
        part = mm(sides[lhs], wides[wide])
        columns = []
        for q in range(W // 4):
            pieces = [
                part[(4 * q + i) * D : (4 * q + i + 1) * D, h * W : (h + 1) * W]
                for i in range(4)
                for h in range(D)
            ]
            columns.append(jnp.concatenate(pieces, axis=0).astype(BF16))
        whole = mm(kron[lhs], jnp.concatenate(columns, axis=1))
        for d in range(D):
            pieces = [
                whole[(i * D + d) * D : (i * D + d + 1) * D, q * W : (q + 1) * W]
                for q in range(W // 4)
                for i in range(4)
            ]
            z[side, :, d * W : (d + 1) * W] = jnp.concatenate(pieces, axis=0).astype(BF16)
        gram = jnp.zeros((W, W), F32)
        for d in range(D):
            piece = z[side, :, d * W : (d + 1) * W]
            gram += mm_tn(piece, piece)
        gram_own[side] = gram

    def send_gram(r, side):
        gram_out[r, side] = gram_own[side].astype(BF16)
        g_copy(r, side).start()

    def masked(block):
        size = sizes_ref[me]
        inside = ((iota((W * D, W), 0) >> 3) < size) & (iota((W * D, W), 1) < size)
        return jnp.where(inside, block.astype(F32), 0.0)

    def turn_side(start, side):
        tall[...] = start
        for u in range(D):
            mid[:, u * W : (u + 1) * W] = tall[pl.ds(u, W, stride=D), :].T
        for u in range(D):
            tall[pl.ds(u, W, stride=D), :] = mid[:, u * W : (u + 1) * W]
        sides[side] = tall[...].astype(BF16)

    def prepare_near():
        near_copy().wait_recv()
        turn_side(masked(near[...]), 2)

    sides[0] = masked(bm[0]).astype(BF16)

    @pl.when(me != 0)
    def _():
        prepare_near()

    @pl.when(me == 3)
    def _():
        for c in range(HOPS):
            hop_in(c).wait_recv()
            hop_on(c).start()

    relay(0)
    prepare_right(0)

    @pl.when(me == 1)
    def _():
        send_sketch(1)

    eye = (iota((W, W), 0) == iota((W, W), 1)).astype(F32)

    def absorb(r, carry):
        first_row = r == 0
        early = jnp.where(first_row, 0, 1 - lax.rem(col, 2))
        absorb_side(early, early, early)

        @pl.when(first_row)
        def _():
            @pl.when(me == 0)
            def _():
                for c in range(HOPS):
                    hop_in(c).wait_send()
                send_sketch(3)
                for c in range(CHUNKS):
                    r_copy(1, c).wait_send()
                for c in range(HOPS, CHUNKS):
                    r_copy(2, c).start()
                near_comp_copy().wait_recv()
                for k in range(1, NS):
                    near_comp_on(k).start()
                prepare_near()

            @pl.when(me != 0)
            def _():
                near_comp_copy().wait_recv()

            expand(near_comp[...].astype(F32), ((1, 2),))

        @pl.when(jnp.logical_not(first_row))
        def _():
            send_gram(r, early)

        absorb_side(
            jnp.where(first_row, 2, 1 - early), jnp.where(first_row, 0, 1 - early), 1 - early
        )

        @pl.when(first_row)
        def _():
            gram_out[0, 0] = (gram_own[0] + gram_own[1]).astype(BF16)
            g_copy(0, 0).start()
            gram_in[0, 1] = gram_own[1].astype(BF16)
            gram_own[1] = jnp.zeros((W, W), F32)

            left_arrives(0)
            l_turned[...] = l_raw[0].astype(F32).T.astype(BF16)

        @pl.when(jnp.logical_not(first_row))
        def _():
            send_gram(r, 1 - early)

        mid[...] = mm(l_turned[...], z[0])

        @pl.when((r == 0) & (me == 1))
        def _():
            send_sketch(2)

        @pl.when((r == 0) & (me == 3))
        def _():
            for k in range(1, NS):
                send_sketch(k)

        @pl.when(r == 0)
        def _():
            relay(1)
            prepare_right(1)

        @pl.when((r > 0) & (r < NS - 1))
        def _():
            left_arrives(r + 1)
            prepare_left(r + 1)
            prepare_right(r + 1)

        g_copy(r, 0).wait_recv()

        @pl.when(r > 0)
        def _():
            g_copy(r, 1).wait_recv()

        for side in range(2):
            work[side, :, :W] = gram_in[r, side].astype(F32) + gram_own[1 - side] + eye
            work[side, :, W:] = eye
        inverse_factors(work, inverse, mixed)

        @pl.when(r < NS - 2)
        def _():
            relay(r + 2)

        @pl.when(r == 0)
        def _():
            left_arrives(1)
            prepare_left(1)

        def solved():
            lefted = mm3(inverse[0], mid[...])
            for d in range(D):
                tall[pl.ds(d, W, stride=D), :] = lefted[:, d * W : (d + 1) * W]
            high, low = halves(inverse[1])
            second = jnp.concatenate([high, low, high], axis=1)
            high, low = halves(tall[...])
            fresh = mm_nt(jnp.concatenate([high, high, low], axis=1), second)
            return lefted, second, fresh, lax.rsqrt(jnp.mean(fresh * fresh) + 1e-6)

        @pl.when(r < NS - 1)
        def _():
            lefted, second, fresh, scaling = solved()
            high, low = halves(lefted)
            for d in range(D):
                lanes_d = slice(d * W, (d + 1) * W)
                piece = jnp.concatenate([high[:, lanes_d], high[:, lanes_d], low[:, lanes_d]], axis=1)
                turned[pl.ds(d, W, stride=D), :] = mm_nt(second, piece)
            result = (fresh * scaling).astype(BF16)
            sides[0] = result
            bm[r + 1] = result
            sides[1] = (turned[...] * scaling).astype(BF16)
            send_result(r)

        @pl.when(r == NS - 1)
        def _():
            _, _, fresh, scaling = solved()
            bm[r + 1] = (fresh * scaling).astype(BF16)
            send_result(r)

        return carry

    lax.fori_loop(0, NS, absorb, 0)

    for c in range(CHUNKS):

        @pl.when(me != 0)
        def _():
            r_copy(1, c).wait_send()

        if c < HOPS:

            @pl.when(me != 0)
            def _():
                r_copy(2, c).wait_send()

            @pl.when(me == 3)
            def _():
                hop_on(c).wait_send()

        else:
            r_copy(2, c).wait_send()
        r_copy(3, c).wait_send()
        for r in range(NS):
            l_copy(r, c).wait_send()
    for k in range(1, NS):
        w_copy(k).wait_send()
    near_copy().wait_send()

    @pl.when(me == 0)
    def _():
        near_comp_copy().wait_send()
        for k in range(1, NS):
            near_comp_on(k).wait_send()

    for r in range(NS):
        g_copy(r, 0).wait_send()
        if r > 0:
            g_copy(r, 1).wait_send()

        @pl.when(r != me)
        def _():
            o_copy(r).wait_send()
            o_arrival(r).wait_recv()

    o_stay(me).wait()


def body(boundary, peps_rows, sketch, ranks, sizes, charges):
    any_space = pl.BlockSpec(memory_space=pl.ANY)
    smem = pl.BlockSpec(memory_space=pltpu.SMEM)
    vmem = pl.BlockSpec(memory_space=pltpu.VMEM)
    dma = pltpu.SemaphoreType.DMA
    result = pl.pallas_call(
        kernel,
        out_shape=pltpu.VMEM((NS, W * D, W), BF16),
        in_specs=[vmem, smem, smem, smem, any_space, any_space],
        out_specs=any_space,
        scratch_shapes=[
            pltpu.VMEM((NS, W * D, W), BF16),
            pltpu.VMEM((NS + 1, W * D, W), BF16),
            pltpu.VMEM((3, W * D, W), BF16),
            pltpu.VMEM((NS, W * D, W), BF16),
            pltpu.VMEM((NS, W * D, W), BF16),
            pltpu.VMEM((2, W, W * D), BF16),
            pltpu.VMEM((W, W * D), BF16),
            pltpu.VMEM((64, W), F32),
            pltpu.VMEM((NS, 64, W), BF16),
            pltpu.VMEM((3, 256, 256), BF16),
            pltpu.VMEM((2, W * D, W * D), BF16),
            pltpu.VMEM((W, W * D), F32),
            pltpu.VMEM((W * D, W), F32),
            pltpu.VMEM((2, W, W), F32),
            pltpu.VMEM((NS, 2, W, W), BF16),
            pltpu.VMEM((NS, 2, W, W), BF16),
            pltpu.VMEM((2, W, 2 * W), F32),
            pltpu.VMEM((2, W, W), F32),
            pltpu.VMEM((2, W, 4 * W), F32),
            pltpu.VMEM((HOPS, CHUNK, W), BF16),
            pltpu.VMEM((W * D, W), BF16),
            pltpu.VMEM((64, W), BF16),
            pltpu.VMEM((W * D, W), F32),
            dma((NS,)), dma(()), dma((NS - 1, CHUNKS)), dma((NS, CHUNKS)), dma((NS - 1,)),
            dma((NS,)), dma((NS, CHUNKS)), dma((NS, CHUNKS)), dma((NS, 2)), dma((NS, 2)),
            dma((NS,)), dma((NS,)), dma(()), dma((HOPS,)), dma((HOPS,)),
            dma((2,)), dma((2,)), dma((NS - 1,)),
        ],
        compiler_params=pltpu.CompilerParams(
            collective_id=0, has_side_effects=True, vmem_limit_bytes=56 * 2**20
        ),
        name="absorb_rows",
    )(
        peps_rows.reshape(D * D, D, D),
        ranks.reshape(NS),
        sizes,
        charges,
        boundary.reshape(NS, W * D, W),
        sketch.reshape(NS, W * D, W),
    )
    return result.reshape(1, 1, NS, W, D, W)


def solution(mesh):
    placed = (
        P("col", None, None, None, None),
        P("row", "col", None, None, None, None),
        P("row", "col", None, None, None),
        P("row", "col", None),
        P(),
        P(),
    )
    return jax.shard_map(
        body,
        mesh=mesh,
        in_specs=placed,
        out_specs=P("row", "col", None, None, None, None),
        check_vma=False,
    )
```
